512 devices in a mesh: front: 8 (over x, core), row: 16 (over z), col: 4 (over y).
Axes of the slice: x: 4, y: 4, z: 16, core: 2. Of those that a mesh axis runs over, the one named last changes fastest.
Arguments:
- child_rhs: float32 [8, 4096, 512], P('front', ('row', 'col')), may hold values from -6 to 6
- pivot_inverse: float32 [8, 4096, 4096], P('front', 'col', 'row')
- border_factor: float32 [8, 4096, 4096], P('front', 'row', 'col'), may hold values from -0.09375 to 0.09375
- front_sizes: int32 [8, 2], P('front'), may hold values from 1024 to 4096, as said below
- border_index: int32 [8, 4096], P('front'), may hold values from 0 to 8191, as said below
- root_rhs: float32 [8192, 512], P('row'), may hold values from -6 to 6
- root_inverse: float32 [8192, 8192], P(('front', 'col'), 'row')
Outputs:
- child_solution: float32 [8, 4096, 512], P('front', 'col', 'row')
- root_solution: float32 [8192, 512], P(('front', 'col'), 'row')
The draws below stay inside these ranges and needn't reach their ends.
Inputs may be any that keep to these rules, and one draw needn't show every extreme that they name: `front_sizes`: row c holds child c's pivot count, from 1024 to 4096, and its border count, from 1024 to 4096; some child has both at 4096 and 4096. `border_index`: for each child, 4096 distinct root rows in no particular order; border row i takes part only if i is below the child's border count.
All inputs are finite; a program needn't handle non-finite values.
Results may differ from the reference program's by a relative error of at most 0.0003.
Values sent between devices are 32-bit elements; how exact they have to be, the bound alone decides.
No kernel may reach another device: no remote copies, remote signals or barrier semaphores. Data moves between devices by JAX's collectives and lax.ppermute only.
A program may use at most 64 MiB of HBM per device.

```python
import math
import jax
import jax.numpy as jnp
from jax import lax

P_SIZE = 4096
B = 4096
R = 8192
S = 512
CHILDREN = 8


def lower_inverse(key, count, leading):
    shape = leading + (count, count)
    values = jax.random.normal(key, shape, jnp.float32) / math.sqrt(count)
    strictly_lower = jnp.arange(count)[:, None] > jnp.arange(count)[None, :]
    return jnp.where(strictly_lower, values, 0.0) + jnp.eye(count, dtype=jnp.float32)


def draw_pivot_inverse(key, part):
    return lower_inverse(key, P_SIZE, (CHILDREN,))


def draw_root_inverse(key, part):
    return lower_inverse(key, R, ())


def draw_front_sizes(key, part):
    key_pivot, key_border, key_chosen = jax.random.split(key, 3)
    pivots = jax.random.randint(key_pivot, (CHILDREN,), P_SIZE // 4, P_SIZE + 1)
    borders = jax.random.randint(key_border, (CHILDREN,), B // 4, B + 1)
    chosen = jax.random.randint(key_chosen, (), 0, CHILDREN)
    largest = jnp.arange(CHILDREN) == chosen
    pivots = jnp.where(largest, P_SIZE, pivots)
    borders = jnp.where(largest, B, borders)
    return jnp.stack([pivots, borders], axis=1).astype(jnp.int32)


def draw_border_index(key, part):
    child_keys = jax.random.split(key, CHILDREN)

    def draw_child(child_key):
        keys = jax.random.split(child_key, 8)
        window = jax.random.randint(keys[0], (), B, R + 1)
        window_start = jax.random.randint(keys[1], (), 0, R - window + 1)
        split_flag = jax.random.randint(keys[2], (), 0, 2)
        gap_length = jax.random.randint(keys[3], (), 0, window - B + 1) * split_flag
        gap_start = window_start + jax.random.randint(keys[4], (), 0, window - gap_length + 1)
        slope = jax.random.randint(keys[5], (), -3, 4)
        root_rows = jnp.arange(R, dtype=jnp.int32)
        in_window = (root_rows >= window_start) & (root_rows < window_start + window)
        in_gap = (root_rows >= gap_start) & (root_rows < gap_start + gap_length)
        inside = in_window & jnp.logical_not(in_gap)
        ramp = slope * ((root_rows - window_start) * 1024 // window) * 1024
        noise = jax.random.randint(keys[6], (R,), 0, 1 << 20)
        score = jnp.where(inside, (1 << 28) + ramp + noise, noise)
        score = jnp.where((root_rows == 0) | (root_rows == R - 1), 1 << 30, score)
        order = jnp.argsort(-score, stable=True)
        chosen_rows = jnp.sort(order[:B])
        return jax.random.permutation(keys[7], chosen_rows)
    return jax.vmap(draw_child)(child_keys).astype(jnp.int32)


def block_levels(own_key, dims, shards, least, top_value):
    gain = 1.0
    for dim, blocks in shards:
        draws = jax.random.uniform(jax.random.fold_in(jax.random.fold_in(own_key, 6), dim), (blocks,), jnp.float32, least / len(shards), top_value / len(shards))
        gain = gain * jnp.repeat(jnp.exp(draws), dims[dim] // blocks).reshape((-1,) + (1,) * (len(dims) - 1 - dim))
    return gain


def gaussian(key, shape, width, bound, shards=(), held_as=jnp.bfloat16):
    loudness = block_levels(key, shape, shards, -0.22, 0.18) if shards else 1.0
    array = jax.random.normal(key, shape, jnp.float32) * width * loudness
    return jnp.minimum(jnp.maximum(array, -bound), bound).astype(held_as)


def setup_inputs(seed: int = 0) -> dict:
    seeds = jax.random.split(jax.random.key(seed), 8)
    return {
        "child_rhs": gaussian(seeds[0], (CHILDREN, P_SIZE, S), 1.0, 6.0, ((0, 8), (1, 64)), jnp.float32),
        "pivot_inverse": draw_pivot_inverse(jax.random.fold_in(seeds[7], 71), 0),
        "border_factor": gaussian(seeds[2], (CHILDREN, B, P_SIZE), P_SIZE ** -0.5, 0.09375, ((0, 8), (1, 16), (2, 4)), jnp.float32),
        "front_sizes": draw_front_sizes(jax.random.fold_in(seeds[7], 71), 0),
        "border_index": draw_border_index(jax.random.fold_in(seeds[7], 71), 0),
        "root_rhs": gaussian(seeds[5], (R, S), 1.0, 6.0, ((0, 16),), jnp.float32),
        "root_inverse": draw_root_inverse(jax.random.fold_in(seeds[7], 71), 0),
    }


def reference(child_rhs, pivot_inverse, border_factor, front_sizes, border_index, root_rhs, root_inverse):
    precise = lax.Precision.HIGHEST

    def one_child(running, inputs_now):
        right_side, inverse_now, border_now, counts_now, index_now = inputs_now
        solved = jnp.dot(inverse_now, right_side, preferred_element_type=jnp.float32, precision=precise)
        solved = jnp.where((jnp.arange(P_SIZE, dtype=jnp.int32) < counts_now[0])[:, None], solved, jnp.zeros_like(solved))
        update = jnp.dot(border_now, solved, preferred_element_type=jnp.float32, precision=precise)
        update = jnp.where((jnp.arange(B, dtype=jnp.int32) < counts_now[1])[:, None], update, jnp.zeros_like(update))
        running = running.at[index_now].add(update)
        return running, solved

    assembled, child_solution = lax.scan(one_child, jnp.zeros((R, S), jnp.float32), (child_rhs, pivot_inverse, border_factor, front_sizes, border_index))
    root_solution = jnp.dot(root_inverse, root_rhs - assembled, preferred_element_type=jnp.float32, precision=precise)
    return child_solution, root_solution
```

```python
import jax
import jax.numpy as jnp
from jax import lax
from jax.sharding import PartitionSpec as P

HIGH = lax.Precision.HIGH


def contract(left, right, left_dims, right_dims):
    return lax.dot_general(
        left,
        right,
        ((left_dims, right_dims), ((), ())),
        precision=HIGH,
        preferred_element_type=jnp.float32,
    )


def exchange(blocks, axes):
    return lax.all_to_all(blocks, axes, split_axis=0, concat_axis=0, tiled=True)


def local(
    child_rhs, pivot_inverse, border_factor, front_sizes, border_index, root_rhs, root_inverse
):
    rows = lax.axis_size("row")
    cols = lax.axis_size("col")
    fronts = lax.axis_size("front")
    layer = fronts * cols
    col_id = lax.axis_index("col")
    row_id = lax.axis_index("row")
    front_id = lax.axis_index("front")
    inverse = pivot_inverse[0]
    border = border_factor[0]
    pivot_rows = inverse.shape[0]
    border_rows = border.shape[0]
    root_rows, sources = root_rhs.shape
    part = sources // layer
    halves = 2
    low_count = rows * halves
    high_count = root_rows // halves

    start = row_id * border_rows
    index = lax.dynamic_slice_in_dim(border_index[0], start, border_rows)
    live = start + jnp.arange(border_rows, dtype=jnp.int32) < front_sizes[0, 1]
    index = lax.all_gather(jnp.where(live, index, -1), "front", axis=0)

    rhs = lax.all_gather(child_rhs[0], "col", axis=0, tiled=True)
    partial = contract(inverse, rhs, (1,), (0,))
    own = lax.psum_scatter(partial, "row", scatter_dimension=1, tiled=True)
    pivot_live = col_id * pivot_rows + jnp.arange(pivot_rows, dtype=jnp.int32) < front_sizes[0, 0]
    own = jnp.where(pivot_live[:, None], own, 0.0)
    solved = lax.all_gather(own, "row", axis=1, tiled=True)

    update = contract(solved, border, (0,), (1,))
    update = exchange(update, ("front", "col"))
    update = update.reshape(fronts, cols, part, border_rows).sum(1)

    low = jnp.where(index < 0, -1, index // high_count)
    high = index % high_count
    at_low = low[None, :, :] == jnp.arange(low_count, dtype=jnp.int32)[:, None, None]
    at_high = high[:, :, None] == jnp.arange(high_count, dtype=jnp.int32)
    spread = jnp.where(at_low[:, None], update.transpose(1, 0, 2)[None], 0.0)
    landed = contract(
        spread.reshape(low_count * part, fronts * border_rows),
        at_high.astype(jnp.float32).reshape(fronts * border_rows, high_count),
        (1,),
        (0,),
    )
    landed = exchange(landed, "row").reshape(rows, halves, part, high_count).sum(0)

    share = front_id * cols + col_id
    rhs_share = lax.dynamic_slice_in_dim(root_rhs, share * part, part, 1)
    rhs_share = rhs_share.reshape(halves, high_count, part).transpose(0, 2, 1)
    residual = rhs_share - landed
    residual = exchange(
        jnp.broadcast_to(residual[None], (layer, halves, part, high_count)), ("front", "col")
    )
    residual = residual.transpose(0, 2, 1, 3).reshape(sources, root_rows)

    root = contract(residual, root_inverse, (1,), (1,))
    root = exchange(root, "row").reshape(rows, sources // rows, root_inverse.shape[0]).sum(0)
    return own[None], root.T


def solution(mesh):
    in_specs = (
        P("front", ("row", "col"), None),
        P("front", "col", "row"),
        P("front", "row", "col"),
        P("front", None),
        P("front", None),
        P("row", None),
        P(("front", "col"), "row"),
    )
    out_specs = (P("front", "col", "row"), P(("front", "col"), "row"))
    return jax.shard_map(local, mesh=mesh, in_specs=in_specs, out_specs=out_specs, check_vma=False)
```

```python
import jax
import jax.numpy as jnp
from jax import lax
from jax.sharding import PartitionSpec as P

HIGH = lax.Precision.HIGH


def contract(left, right, left_dims, right_dims):
    return lax.dot_general(
        left,
        right,
        ((left_dims, right_dims), ((), ())),
        precision=HIGH,
        preferred_element_type=jnp.float32,
    )


def exchange(blocks, axes):
    return lax.all_to_all(blocks, axes, split_axis=0, concat_axis=0, tiled=True)


def local(
    child_rhs, pivot_inverse, border_factor, front_sizes, border_index, root_rhs, root_inverse
):
    rows = lax.axis_size("row")
    cols = lax.axis_size("col")
    fronts = lax.axis_size("front")
    layer = fronts * cols
    col_id = lax.axis_index("col")
    row_id = lax.axis_index("row")
    front_id = lax.axis_index("front")
    inverse = pivot_inverse[0]
    border = border_factor[0]
    pivot_rows = inverse.shape[0]
    border_rows = border.shape[0]
    root_rows, sources = root_rhs.shape
    part = sources // layer
    halves = 2
    low_count = rows * halves
    high_count = root_rows // halves

    start = row_id * border_rows
    index = lax.dynamic_slice_in_dim(border_index[0], start, border_rows)
    live = start + jnp.arange(border_rows, dtype=jnp.int32) < front_sizes[0, 1]
    index = jnp.where(live, index, -1)

    near = 4
    far = rows // near
    block = sources // rows
    step = 1 - 2 * lax.rem(front_id, 2)

    def shift(value, distance, mirrored=True):
        pairs = []
        for front in range(fronts):
            by = -distance if mirrored and front % 2 else distance
            pairs += [(front * rows + z, front * rows + (z + by) % rows) for z in range(rows)]
        return lax.ppermute(value, ("front", "row"), pairs)

    def group_at(offset):
        return lax.rem(row_id + offset + near, near)

    rhs = child_rhs[0].reshape(-1, far, near, block).transpose(2, 0, 1, 3)
    rhs = rhs.reshape(near, -1, far * block)
    rhs = jnp.stack(
        [
            lax.dynamic_index_in_dim(rhs, group_at(offset), 0, keepdims=False)
            for offset in (2, step, -step, 0)
        ]
    )
    rhs = lax.all_gather(rhs, "col", axis=1, tiled=True)

    def pivot_product(which):
        return contract(rhs[which], inverse, (0,), (1,))

    from_two = shift(pivot_product(0), -1)
    below, index = lax.optimization_barrier((pivot_product(1), index))
    from_below = shift(below, 1)
    index = lax.all_gather(index, "front", axis=0)
    from_two, index = lax.optimization_barrier((from_two, index))
    from_above = shift(pivot_product(2) + from_two, -1)
    near_sum = pivot_product(3) + from_below + from_above
    near_sum = near_sum.reshape(far, block, pivot_rows)
    far_id = lax.div(row_id, near)

    def far_block(offset):
        return lax.dynamic_index_in_dim(near_sum, lax.rem(far_id + offset, far), 0, keepdims=False)

    own = far_block(0)
    for offset in range(1, far):
        own = own + shift(far_block(offset), offset * near, False)
    pivot_live = col_id * pivot_rows + jnp.arange(pivot_rows, dtype=jnp.int32) < front_sizes[0, 0]
    own = jnp.where(pivot_live[None, :], own, 0.0)

    apart = [[g + near * i for i in range(far)] for g in range(near)]
    solved = lax.all_gather(own, "row", axis_index_groups=apart, axis=0, tiled=True)
    solved_above = shift(solved, -1)
    solved_below = shift(solved, 1)
    solved_two = shift(solved_above, -1)
    update = jnp.zeros((near, far * block, border_rows), jnp.float32)
    for value, offset in (
        (solved, 0), (solved_above, step), (solved_below, -step), (solved_two, 2)
    ):
        piece = contract(value, border, (1,), (1,))
        update = lax.dynamic_update_slice_in_dim(update, piece[None], group_at(offset), 0)
    update = update.reshape(sources, border_rows)
    update = exchange(update, ("front", "col"))
    update = update.reshape(fronts, cols, part, border_rows).sum(1)

    low = jnp.where(index < 0, -1, index // high_count)
    high = index % high_count
    at_low = low[None, :, :] == jnp.arange(low_count, dtype=jnp.int32)[:, None, None]
    at_high = high[:, :, None] == jnp.arange(high_count, dtype=jnp.int32)
    spread = jnp.where(at_low[:, None], update.transpose(1, 0, 2)[None], 0.0)
    landed = contract(
        spread.reshape(low_count * part, fronts * border_rows),
        at_high.astype(jnp.float32).reshape(fronts * border_rows, high_count),
        (1,),
        (0,),
    )
    landed = exchange(landed, "row").reshape(rows, halves, part, high_count).sum(0)

    share = front_id * cols + col_id
    per_block = block // part
    in_block = lax.rem(share, per_block)
    far_share = lax.rem(lax.div(share, per_block), far)
    near_share = lax.div(share, per_block * far)
    first = (far_share * near + near_share) * block + in_block * part
    rhs_share = lax.dynamic_slice_in_dim(root_rhs, first, part, 1)
    rhs_share = rhs_share.reshape(halves, high_count, part).transpose(0, 2, 1)
    residual = rhs_share - landed
    residual = exchange(
        jnp.broadcast_to(residual[None], (layer, halves, part, high_count)), ("front", "col")
    )
    residual = residual.reshape(near, far, per_block, halves, part, high_count)
    residual = residual.transpose(1, 0, 2, 4, 3, 5).reshape(sources, root_rows)

    root = contract(residual, root_inverse, (1,), (1,))
    root = exchange(root, "row").reshape(rows, sources // rows, root_inverse.shape[0]).sum(0)
    return own.T[None], root.T


def solution(mesh):
    in_specs = (
        P("front", ("row", "col"), None),
        P("front", "col", "row"),
        P("front", "row", "col"),
        P("front", None),
        P("front", None),
        P("row", None),
        P(("front", "col"), "row"),
    )
    out_specs = (P("front", "col", "row"), P(("front", "col"), "row"))
    return jax.shard_map(local, mesh=mesh, in_specs=in_specs, out_specs=out_specs, check_vma=False)
```

```python
import functools

import jax
import jax.numpy as jnp
from jax import lax
from jax.experimental import pallas as pl
from jax.experimental.pallas import tpu as pltpu
from jax.sharding import PartitionSpec as P

HIGH = lax.Precision.HIGH


def contract(left, right, left_dims, right_dims):
    return lax.dot_general(
        left,
        right,
        ((left_dims, right_dims), ((), ())),
        precision=HIGH,
        preferred_element_type=jnp.float32,
    )


def exchange(blocks, axes):
    return lax.all_to_all(blocks, axes, split_axis=0, concat_axis=0, tiled=True)


def land_kernel(fronts, cols, update_ref, place_ref, high_ref, out_ref):
    part, border_rows = update_ref.shape[1:]
    places = out_ref.shape[0] // part
    high_count = out_ref.shape[1]
    place_iota = lax.broadcasted_iota(jnp.int32, (places, 1, border_rows), 0)
    high_iota = lax.broadcasted_iota(jnp.int32, (high_count, border_rows), 0)
    fronts_a_step = 2
    for base in range(0, fronts, fronts_a_step):
        left, right = [], []
        for front in range(base, base + fronts_a_step):
            value = update_ref[front * cols]
            for col in range(1, cols):
                value = value + update_ref[front * cols + col]
            coarse = value.astype(jnp.bfloat16).astype(jnp.float32)
            at_high = jnp.where(high_iota == high_ref[front], 1.0, 0.0).astype(jnp.bfloat16)
            at_place = place_iota == place_ref[front][None]
            for piece in (coarse, value - coarse):
                spread = jnp.where(at_place, piece[None], 0.0)
                left.append(spread.reshape(places * part, border_rows).astype(jnp.bfloat16))
                right.append(at_high)
        landed = lax.dot_general(
            jnp.concatenate(left, 1),
            jnp.concatenate(right, 1),
            (((1,), (1,)), ((), ())),
            preferred_element_type=jnp.float32,
        )
        if base == 0:
            out_ref[...] = landed
        else:
            out_ref[...] += landed


def land(update, place, high, fronts, cols, places, high_count):
    part, border_rows = update.shape[1:]
    out = jax.ShapeDtypeStruct((places * part, high_count), jnp.float32)
    return pl.pallas_call(
        functools.partial(land_kernel, fronts, cols),
        out_shape=out,
        in_specs=[pl.BlockSpec(memory_space=pltpu.VMEM)] * 3,
        out_specs=pl.BlockSpec(memory_space=pltpu.VMEM),
        compiler_params=pltpu.CompilerParams(vmem_limit_bytes=32 * 1024 * 1024),
        cost_estimate=pl.CostEstimate(
            flops=4 * places * part * high_count * fronts * border_rows,
            bytes_accessed=4 * (update.size + places * part * high_count),
            transcendentals=0,
        ),
    )(update, place[:, None], high[:, None])


def local(
    child_rhs, pivot_inverse, border_factor, front_sizes, border_index, root_rhs, root_inverse
):
    rows = lax.axis_size("row")
    cols = lax.axis_size("col")
    fronts = lax.axis_size("front")
    layer = fronts * cols
    col_id = lax.axis_index("col")
    row_id = lax.axis_index("row")
    front_id = lax.axis_index("front")
    inverse = pivot_inverse[0]
    border = border_factor[0]
    pivot_rows = inverse.shape[0]
    border_rows = border.shape[0]
    root_rows, sources = root_rhs.shape
    part = sources // layer
    halves = 2
    low_count = rows * halves
    high_count = root_rows // halves

    start = row_id * border_rows
    index = lax.dynamic_slice_in_dim(border_index[0], start, border_rows)
    live = start + jnp.arange(border_rows, dtype=jnp.int32) < front_sizes[0, 1]
    index = jnp.where(live, index, -1)

    near = 4
    far = rows // near
    block = sources // rows
    step = 1 - 2 * lax.rem(front_id, 2)

    def shift(value, distance, mirrored=True):
        pairs = []
        for front in range(fronts):
            by = -distance if mirrored and front % 2 else distance
            pairs += [(front * rows + z, front * rows + (z + by) % rows) for z in range(rows)]
        return lax.ppermute(value, ("front", "row"), pairs)

    def row_sum(blocks):
        parity = lax.rem(row_id, 2)
        pairs = []
        for front in range(fronts):
            by = front % 2
            pairs += [
                (front * rows + z, front * rows + (((z + by) ^ 1) - by) % rows) for z in range(rows)
            ]
        theirs = lax.dynamic_index_in_dim(blocks, 1 - parity, 0, keepdims=False)
        mine = lax.dynamic_index_in_dim(blocks, parity, 0, keepdims=False)
        mine = mine + lax.ppermute(theirs, ("front", "row"), pairs)
        same = [list(range(first, rows, 2)) for first in (0, 1)]
        mine = lax.all_to_all(mine, "row", 0, 0, axis_index_groups=same, tiled=True)
        return mine.sum(0)

    def group_at(offset):
        return lax.rem(row_id + offset + near, near)

    rhs = child_rhs[0].reshape(-1, far, near, block).transpose(2, 0, 1, 3)
    rhs = rhs.reshape(near, -1, far * block)
    rhs = jnp.stack(
        [
            lax.dynamic_index_in_dim(rhs, group_at(offset), 0, keepdims=False)
            for offset in (2, step, -step, 0)
        ]
    )
    rhs = lax.all_gather(rhs, "col", axis=1, tiled=True)

    def pivot_product(which):
        return contract(rhs[which], inverse, (0,), (1,))

    from_two = shift(pivot_product(0), -1)
    below, index = lax.optimization_barrier((pivot_product(1), index))
    from_below = shift(below, 1)
    index = lax.all_gather(index, "front", axis=0)
    from_two, index = lax.optimization_barrier((from_two, index))
    from_above = shift(pivot_product(2) + from_two, -1)
    near_sum = pivot_product(3) + from_below + from_above
    near_sum = near_sum.reshape(far, block, pivot_rows)
    far_id = lax.div(row_id, near)

    def far_block(offset):
        return lax.dynamic_index_in_dim(near_sum, lax.rem(far_id + offset, far), 0, keepdims=False)

    own = far_block(0)
    for offset in range(1, far):
        own = own + shift(far_block(offset), offset * near, False)
    pivot_live = col_id * pivot_rows + jnp.arange(pivot_rows, dtype=jnp.int32) < front_sizes[0, 0]
    own = jnp.where(pivot_live[None, :], own, 0.0)

    apart = [[g + near * i for i in range(far)] for g in range(near)]
    solved = lax.all_gather(own, "row", axis_index_groups=apart, axis=0, tiled=True)
    solved_above = shift(solved, -1)
    solved_below = shift(solved, 1)
    solved_two = shift(solved_above, -1)
    update = jnp.zeros((near, far * block, border_rows), jnp.float32)
    for value, offset in (
        (solved, 0), (solved_above, step), (solved_below, -step), (solved_two, 2)
    ):
        piece = contract(value, border, (1,), (1,))
        update = lax.dynamic_update_slice_in_dim(update, piece[None], group_at(offset), 0)
    update = update.reshape(sources, border_rows)
    update = exchange(update.reshape(layer, part, border_rows), ("front", "col"))

    low = jnp.where(index < 0, -1, lax.div(index, high_count))
    owner = lax.div(low, halves)
    place = lax.rem(owner, 2) * (low_count // 2) + lax.div(owner, 2) * halves + lax.rem(low, halves)
    place = jnp.where(index < 0, -1, place)
    high = lax.rem(index, high_count)
    landed = land(update, place, high, fronts, cols, low_count, high_count)
    landed = row_sum(landed.reshape(2, rows // 2, halves, part, high_count))

    share = front_id * cols + col_id
    per_block = block // part
    in_block = lax.rem(share, per_block)
    far_share = lax.rem(lax.div(share, per_block), far)
    near_share = lax.div(share, per_block * far)
    first = (far_share * near + near_share) * block + in_block * part
    rhs_share = lax.dynamic_slice_in_dim(root_rhs, first, part, 1)
    rhs_share = rhs_share.reshape(halves, high_count, part).transpose(0, 2, 1)
    residual = rhs_share - landed
    residual = exchange(
        jnp.broadcast_to(residual[None], (layer, halves, part, high_count)), ("front", "col")
    )
    residual = residual.reshape(near // 2, 2, far, per_block, halves, part, high_count)
    residual = residual.transpose(1, 2, 0, 3, 5, 4, 6).reshape(sources, root_rows)

    root = contract(residual, root_inverse, (1,), (1,))
    root = row_sum(root.reshape(2, rows // 2, block, root_inverse.shape[0]))
    return own.T[None], root.T


def solution(mesh):
    in_specs = (
        P("front", ("row", "col"), None),
        P("front", "col", "row"),
        P("front", "row", "col"),
        P("front", None),
        P("front", None),
        P("row", None),
        P(("front", "col"), "row"),
    )
    out_specs = (P("front", "col", "row"), P(("front", "col"), "row"))
    return jax.shard_map(local, mesh=mesh, in_specs=in_specs, out_specs=out_specs, check_vma=False)
```

```python
import functools

import jax
import jax.numpy as jnp
from jax import lax
from jax.experimental import pallas as pl
from jax.experimental.pallas import tpu as pltpu
from jax.sharding import PartitionSpec as P

HIGH = lax.Precision.HIGH


def contract(left, right, left_dims, right_dims):
    return lax.dot_general(
        left,
        right,
        ((left_dims, right_dims), ((), ())),
        precision=HIGH,
        preferred_element_type=jnp.float32,
    )


def exchange(blocks, axes):
    return lax.all_to_all(blocks, axes, split_axis=0, concat_axis=0, tiled=True)


def land_kernel(fronts, cols, update_ref, place_ref, high_ref, out_ref):
    part, border_rows = update_ref.shape[1:]
    places = out_ref.shape[0] // part
    high_count = out_ref.shape[1]
    place_iota = lax.broadcasted_iota(jnp.int32, (places, 1, border_rows), 0)
    high_iota = lax.broadcasted_iota(jnp.int32, (high_count, border_rows), 0)
    fronts_a_step = 2
    for base in range(0, fronts, fronts_a_step):
        left, right = [], []
        for front in range(base, base + fronts_a_step):
            value = update_ref[front * cols]
            for col in range(1, cols):
                value = value + update_ref[front * cols + col]
            coarse = value.astype(jnp.bfloat16).astype(jnp.float32)
            at_high = jnp.where(high_iota == high_ref[front], 1.0, 0.0).astype(jnp.bfloat16)
            at_place = place_iota == place_ref[front][None]
            for piece in (coarse, value - coarse):
                spread = jnp.where(at_place, piece[None], 0.0)
                left.append(spread.reshape(places * part, border_rows).astype(jnp.bfloat16))
                right.append(at_high)
        landed = lax.dot_general(
            jnp.concatenate(left, 1),
            jnp.concatenate(right, 1),
            (((1,), (1,)), ((), ())),
            preferred_element_type=jnp.float32,
        )
        if base == 0:
            out_ref[...] = landed
        else:
            out_ref[...] += landed


def land(update, place, high, fronts, cols, places, high_count):
    part, border_rows = update.shape[1:]
    out = jax.ShapeDtypeStruct((places * part, high_count), jnp.float32)
    return pl.pallas_call(
        functools.partial(land_kernel, fronts, cols),
        out_shape=out,
        in_specs=[pl.BlockSpec(memory_space=pltpu.VMEM)] * 3,
        out_specs=pl.BlockSpec(memory_space=pltpu.VMEM),
        compiler_params=pltpu.CompilerParams(vmem_limit_bytes=32 * 1024 * 1024),
        cost_estimate=pl.CostEstimate(
            flops=4 * places * part * high_count * fronts * border_rows,
            bytes_accessed=4 * (update.size + places * part * high_count),
            transcendentals=0,
        ),
    )(update, place[:, None], high[:, None])


def local(
    child_rhs, pivot_inverse, border_factor, front_sizes, border_index, root_rhs, root_inverse
):
    rows = lax.axis_size("row")
    cols = lax.axis_size("col")
    fronts = lax.axis_size("front")
    layer = fronts * cols
    col_id = lax.axis_index("col")
    row_id = lax.axis_index("row")
    front_id = lax.axis_index("front")
    inverse = pivot_inverse[0]
    border = border_factor[0]
    pivot_rows = inverse.shape[0]
    border_rows = border.shape[0]
    root_rows, sources = root_rhs.shape
    part = sources // layer
    halves = 2
    low_count = rows * halves
    high_count = root_rows // halves

    start = row_id * border_rows
    index = lax.dynamic_slice_in_dim(border_index[0], start, border_rows)
    live = start + jnp.arange(border_rows, dtype=jnp.int32) < front_sizes[0, 1]
    index = jnp.where(live, index, -1)

    near = 8
    far = rows // near
    down = near // 2
    up = near - 1 - down
    block = sources // rows
    step = 1 - 2 * lax.rem(front_id, 2)

    def shift(value, distance, mirrored=True):
        pairs = []
        for front in range(fronts):
            by = -distance if mirrored and front % 2 else distance
            pairs += [(front * rows + z, front * rows + (z + by) % rows) for z in range(rows)]
        return lax.ppermute(value, ("front", "row"), pairs)

    def row_sum(blocks):
        parity = lax.rem(row_id, 2)
        pairs = []
        for front in range(fronts):
            by = front % 2
            pairs += [
                (front * rows + z, front * rows + (((z + by) ^ 1) - by) % rows) for z in range(rows)
            ]
        theirs = lax.dynamic_index_in_dim(blocks, 1 - parity, 0, keepdims=False)
        mine = lax.dynamic_index_in_dim(blocks, parity, 0, keepdims=False)
        mine = mine + lax.ppermute(theirs, ("front", "row"), pairs)
        same = [list(range(first, rows, 2)) for first in (0, 1)]
        mine = lax.all_to_all(mine, "row", 0, 0, axis_index_groups=same, tiled=True)
        return mine.sum(0)

    def group_at(offset):
        return lax.rem(row_id + offset + near, near)

    hops = []
    for hop in range(down):
        hops.append(("down", -step * (down - hop)))
        if hop < up:
            hops.append(("up", step * (up - hop)))
    groups = child_rhs[0].reshape(-1, far, near, block)
    first = lax.dynamic_index_in_dim(groups, group_at(hops[0][1]), 2, keepdims=False)
    first = lax.all_gather(first.reshape(-1, far * block), "col", axis=0, tiled=True)
    first = contract(first, inverse, (0,), (1,))

    first, rhs = lax.optimization_barrier((first, child_rhs[0]))
    running = {"down": shift(first, -1)}
    rhs = lax.all_gather(rhs, "col", axis=0, tiled=True)
    rhs = rhs.T.reshape(far, near, block, -1).transpose(1, 0, 2, 3)
    rhs = rhs.reshape(near, far * block, -1)

    def pivot_product(offset):
        value = lax.dynamic_index_in_dim(rhs, group_at(offset), 0, keepdims=False)
        return contract(value, inverse, (1,), (1,))

    for way, offset in hops[1:]:
        value = pivot_product(offset)
        if way in running:
            value = value + running[way]
        running[way] = shift(value, -1 if way == "down" else 1)
    near_sum = pivot_product(0) + running["down"] + running["up"]
    near_sum = near_sum.reshape(far, block, pivot_rows)
    far_id = lax.div(row_id, near)

    def far_block(offset):
        return lax.dynamic_index_in_dim(near_sum, lax.rem(far_id + offset, far), 0, keepdims=False)

    own = far_block(0)
    away, index = lax.optimization_barrier((far_block(1), index))
    away = shift(away, near, False)
    index = lax.all_gather(index, "front", axis=0)
    away, index = lax.optimization_barrier((away, index))
    pivot_live = col_id * pivot_rows + jnp.arange(pivot_rows, dtype=jnp.int32) < front_sizes[0, 0]
    own = jnp.where(pivot_live[None, :], own + away, 0.0)

    away = shift(own, near, False)
    solved = jnp.where(far_id == 0, jnp.stack([own, away]), jnp.stack([away, own]))
    solved = solved.reshape(far * block, pivot_rows)
    update = jnp.zeros((near, far * block, border_rows), jnp.float32)

    def place_product(update, value, offset):
        piece = contract(value, border, (1,), (1,))
        return lax.dynamic_update_slice_in_dim(update, piece[None], group_at(offset), 0)

    above, below = solved, solved
    arrived = [(solved, 0)]
    for hop in range(1, down + 1):
        above = shift(above, -1)
        arrived.append((above, step * hop))
        if hop <= up:
            below = shift(below, 1)
            arrived.append((below, -step * hop))
    for value, offset in arrived:
        update = place_product(update, value, offset)
    update = exchange(update.reshape(layer, part, border_rows), ("front", "col"))

    low = jnp.where(index < 0, -1, lax.div(index, high_count))
    owner = lax.div(low, halves)
    place = lax.rem(owner, 2) * (low_count // 2) + lax.div(owner, 2) * halves + lax.rem(low, halves)
    place = jnp.where(index < 0, -1, place)
    high = lax.rem(index, high_count)
    landed = land(update, place, high, fronts, cols, low_count, high_count)
    landed = row_sum(landed.reshape(2, rows // 2, halves, part, high_count))

    share = front_id * cols + col_id
    per_block = block // part
    in_block = lax.rem(share, per_block)
    far_share = lax.rem(lax.div(share, per_block), far)
    near_share = lax.div(share, per_block * far)
    first = (far_share * near + near_share) * block + in_block * part
    rhs_share = lax.dynamic_slice_in_dim(root_rhs, first, part, 1)
    rhs_share = rhs_share.reshape(halves, high_count, part).transpose(0, 2, 1)
    residual = rhs_share - landed
    residual = exchange(
        jnp.broadcast_to(residual[None], (layer, halves, part, high_count)), ("front", "col")
    )
    residual = residual.reshape(near // 2, 2, far, per_block, halves, part, high_count)
    residual = residual.transpose(1, 2, 0, 3, 5, 4, 6).reshape(sources, root_rows)

    root = contract(residual, root_inverse, (1,), (1,))
    root = row_sum(root.reshape(2, rows // 2, block, root_inverse.shape[0]))
    return own.T[None], root.T


def solution(mesh):
    in_specs = (
        P("front", ("row", "col"), None),
        P("front", "col", "row"),
        P("front", "row", "col"),
        P("front", None),
        P("front", None),
        P("row", None),
        P(("front", "col"), "row"),
    )
    out_specs = (P("front", "col", "row"), P(("front", "col"), "row"))
    return jax.shard_map(local, mesh=mesh, in_specs=in_specs, out_specs=out_specs, check_vma=False)
```

```python
import functools

import jax
import jax.numpy as jnp
from jax import lax
from jax.experimental import pallas as pl
from jax.experimental.pallas import tpu as pltpu
from jax.sharding import PartitionSpec as P

HIGH = lax.Precision.HIGH


def contract(left, right, left_dims, right_dims):
    return lax.dot_general(
        left,
        right,
        ((left_dims, right_dims), ((), ())),
        precision=HIGH,
        preferred_element_type=jnp.float32,
    )


def exchange(blocks, axes):
    return lax.all_to_all(blocks, axes, split_axis=0, concat_axis=0, tiled=True)


def land_kernel(fronts, cols, update_ref, place_ref, high_ref, out_ref):
    part, border_rows = update_ref.shape[1:]
    out_rows, high_count = out_ref.shape
    places = out_rows // part
    repeats = max(1, 8 // part)
    shape = (places // repeats, repeats * part, border_rows)
    place_iota = lax.broadcasted_iota(jnp.int32, shape, 0) * repeats
    place_iota = place_iota + lax.broadcasted_iota(jnp.int32, shape, 1) // part
    high_iota = lax.broadcasted_iota(jnp.int32, (high_count, border_rows), 0)
    total = None
    for front in range(fronts):
        value = update_ref[front * cols]
        for col in range(1, cols):
            value = value + update_ref[front * cols + col]
        value = jnp.concatenate([value] * repeats, 0)
        coarse = value.astype(jnp.bfloat16).astype(jnp.float32)
        at_high = jnp.where(high_iota == high_ref[front], 1.0, 0.0).astype(jnp.bfloat16)
        at_place = place_iota == place_ref[front][None]
        pieces = []
        for piece in (coarse, value - coarse):
            spread = jnp.where(at_place, piece[None], 0.0)
            pieces.append(spread.reshape(out_rows, border_rows).astype(jnp.bfloat16))
        landed = lax.dot_general(
            jnp.concatenate(pieces, 0),
            at_high,
            (((1,), (1,)), ((), ())),
            preferred_element_type=jnp.float32,
        )
        landed = landed[:out_rows] + landed[out_rows:]
        total = landed if total is None else total + landed
    out_ref[...] = total


def land(update, place, high, fronts, cols, places, high_count):
    part, border_rows = update.shape[1:]
    return pl.pallas_call(
        functools.partial(land_kernel, fronts, cols),
        out_shape=jax.ShapeDtypeStruct((places * part, high_count), jnp.float32),
        in_specs=[pl.BlockSpec(memory_space=pltpu.VMEM)] * 3,
        out_specs=pl.BlockSpec(memory_space=pltpu.VMEM),
        compiler_params=pltpu.CompilerParams(vmem_limit_bytes=32 * 1024 * 1024),
        cost_estimate=pl.CostEstimate(
            flops=4 * places * part * high_count * fronts * border_rows,
            bytes_accessed=4 * (update.size + places * part * high_count),
            transcendentals=0,
        ),
    )(update, place[:, None], high[:, None])


def local(
    child_rhs, pivot_inverse, border_factor, front_sizes, border_index, root_rhs, root_inverse
):
    rows = lax.axis_size("row")
    cols = lax.axis_size("col")
    fronts = lax.axis_size("front")
    layer = fronts * cols
    col_id = lax.axis_index("col")
    row_id = lax.axis_index("row")
    front_id = lax.axis_index("front")
    inverse = pivot_inverse[0]
    border = border_factor[0]
    pivot_rows = inverse.shape[0]
    border_rows = border.shape[0]
    root_rows, sources = root_rhs.shape
    near = 4
    part = sources // near // layer
    halves = 2
    low_count = rows * halves
    high_count = root_rows // halves

    far = rows // near
    block = sources // rows
    step = 1 - 2 * lax.rem(front_id, 2)

    def shift(value, distance, mirrored=True):
        pairs = []
        for front in range(fronts):
            by = -distance if mirrored and front % 2 else distance
            pairs += [(front * rows + z, front * rows + (z + by) % rows) for z in range(rows)]
        return lax.ppermute(value, ("front", "row"), pairs)

    def row_sum(blocks):
        parity = lax.rem(row_id, 2)
        pairs = []
        for front in range(fronts):
            by = front % 2
            pairs += [
                (front * rows + z, front * rows + (((z + by) ^ 1) - by) % rows) for z in range(rows)
            ]
        theirs = lax.dynamic_index_in_dim(blocks, 1 - parity, 0, keepdims=False)
        mine = lax.dynamic_index_in_dim(blocks, parity, 0, keepdims=False)
        mine = mine + lax.ppermute(theirs, ("front", "row"), pairs)
        same = [list(range(first, rows, 2)) for first in (0, 1)]
        mine = lax.all_to_all(mine, "row", 0, 0, axis_index_groups=same, tiled=True)
        return mine.sum(0)

    def group_at(offset):
        return lax.rem(row_id + offset + near, near)

    index = []
    for offset in (0, step, -step, 2 * step):
        start = lax.rem(row_id + offset + rows, rows) * border_rows
        live = start + jnp.arange(border_rows, dtype=jnp.int32) < front_sizes[0, 1]
        piece = lax.dynamic_slice_in_dim(border_index[0], start, border_rows)
        index.append(jnp.where(live, piece, -1))
    index = jnp.concatenate(index)

    rhs = child_rhs[0].reshape(-1, far, near, block).transpose(2, 0, 1, 3)
    rhs = rhs.reshape(near, -1, far * block)
    rhs = jnp.stack(
        [
            lax.dynamic_index_in_dim(rhs, group_at(offset), 0, keepdims=False)
            for offset in (2, step, -step, 0)
        ]
    )
    border_above = shift(border, -1)
    rhs = lax.all_gather(rhs, "col", axis=1, tiled=True)
    rhs, border_above = lax.optimization_barrier((rhs, border_above))

    def pivot_product(which):
        return contract(rhs[which], inverse, (0,), (1,))

    from_two = shift(pivot_product(0), -1)
    from_below = shift(pivot_product(1), 1)
    above, border_sent = lax.optimization_barrier((pivot_product(2) + from_two, border))
    from_above = shift(above, -1)
    border_below = shift(border_sent, 1)
    near_sum = pivot_product(3) + from_below + from_above
    near_sum = near_sum.reshape(far, block, pivot_rows)
    far_id = lax.div(row_id, near)

    def far_block(offset):
        return lax.dynamic_index_in_dim(near_sum, lax.rem(far_id + offset, far), 0, keepdims=False)

    own = far_block(0)
    sent = [far_block(offset) for offset in range(1, far)]
    *sent, index, border_sent = lax.optimization_barrier((*sent, index, border_above))
    sent = [shift(value, near * (1 + hop), False) for hop, value in enumerate(sent)]
    border_two = shift(border_sent, -1)
    index = lax.all_gather(index, "front", axis=0)
    *sent, index = lax.optimization_barrier((*sent, index))
    for value in sent:
        own = own + value
    pivot_live = col_id * pivot_rows + jnp.arange(pivot_rows, dtype=jnp.int32) < front_sizes[0, 0]
    own = jnp.where(pivot_live[None, :], own, 0.0)

    apart = [[g + near * i for i in range(far)] for g in range(near)]
    solved = lax.all_gather(own, "row", axis_index_groups=apart, axis=0, tiled=True)
    window = (border, border_above, border_below, border_two)
    update = jnp.concatenate([contract(solved, value, (1,), (1,)) for value in window], 1)
    update = exchange(update.reshape(layer, part, near * border_rows), ("front", "col"))

    place = jnp.where(index < 0, -1, lax.div(index, high_count))
    high = lax.rem(index, high_count)
    landed = land(update, place, high, fronts, cols, low_count, high_count)
    landed = exchange(landed.reshape(rows, halves * part, high_count), "row")
    landed = landed.reshape(far, near, halves, part, high_count).sum(0)

    share = front_id * cols + col_id
    per_block = layer // far
    rhs_share = root_rhs.reshape(root_rows, far, near, per_block, part)
    rhs_share = lax.dynamic_index_in_dim(rhs_share, lax.div(share, per_block), 1, keepdims=False)
    rhs_share = lax.dynamic_index_in_dim(rhs_share, lax.rem(share, per_block), 2, keepdims=False)
    rhs_share = rhs_share.reshape(halves, high_count, near, part).transpose(2, 0, 3, 1)
    residual = rhs_share - landed
    residual = exchange(
        jnp.broadcast_to(residual[None], (layer, near, halves, part, high_count)), ("front", "col")
    )
    residual = residual.reshape(far, per_block, near // 2, 2, halves, part, high_count)
    residual = residual.transpose(3, 0, 2, 1, 5, 4, 6).reshape(sources, root_rows)

    root = contract(residual, root_inverse, (1,), (1,))
    root = row_sum(root.reshape(2, rows // 2, block, root_inverse.shape[0]))
    return own.T[None], root.T


def solution(mesh):
    in_specs = (
        P("front", ("row", "col"), None),
        P("front", "col", "row"),
        P("front", "row", "col"),
        P("front", None),
        P("front", None),
        P("row", None),
        P(("front", "col"), "row"),
    )
    out_specs = (P("front", "col", "row"), P(("front", "col"), "row"))
    return jax.shard_map(local, mesh=mesh, in_specs=in_specs, out_specs=out_specs, check_vma=False)
```

```python
import functools

import jax
import jax.numpy as jnp
from jax import lax
from jax.experimental import pallas as pl
from jax.experimental.pallas import tpu as pltpu
from jax.sharding import PartitionSpec as P

HIGH = lax.Precision.HIGH


def contract(left, right, left_dims, right_dims):
    return lax.dot_general(
        left,
        right,
        ((left_dims, right_dims), ((), ())),
        precision=HIGH,
        preferred_element_type=jnp.float32,
    )


def exchange(blocks, axes):
    return lax.all_to_all(blocks, axes, split_axis=0, concat_axis=0, tiled=True)


def land_kernel(fronts, cols, update_ref, place_ref, high_ref, out_ref):
    part, border_rows = update_ref.shape[1:]
    out_rows, high_count = out_ref.shape
    places = out_rows // part
    repeats = max(1, 8 // part)
    shape = (places // repeats, repeats * part, border_rows)
    place_iota = lax.broadcasted_iota(jnp.int32, shape, 0) * repeats
    place_iota = place_iota + lax.broadcasted_iota(jnp.int32, shape, 1) // part
    high_iota = lax.broadcasted_iota(jnp.int32, (high_count, border_rows), 0)
    total = None
    for front in range(fronts):
        value = update_ref[front * cols]
        for col in range(1, cols):
            value = value + update_ref[front * cols + col]
        value = jnp.concatenate([value] * repeats, 0)
        coarse = value.astype(jnp.bfloat16).astype(jnp.float32)
        at_high = jnp.where(high_iota == high_ref[front], 1.0, 0.0).astype(jnp.bfloat16)
        at_place = place_iota == place_ref[front][None]
        pieces = []
        for piece in (coarse, value - coarse):
            spread = jnp.where(at_place, piece[None], 0.0)
            pieces.append(spread.reshape(out_rows, border_rows).astype(jnp.bfloat16))
        landed = lax.dot_general(
            jnp.concatenate(pieces, 0),
            at_high,
            (((1,), (1,)), ((), ())),
            preferred_element_type=jnp.float32,
        )
        landed = landed[:out_rows] + landed[out_rows:]
        total = landed if total is None else total + landed
    out_ref[...] = total


def land(update, place, high, fronts, cols, places, high_count):
    part, border_rows = update.shape[1:]
    return pl.pallas_call(
        functools.partial(land_kernel, fronts, cols),
        out_shape=jax.ShapeDtypeStruct((places * part, high_count), jnp.float32),
        in_specs=[pl.BlockSpec(memory_space=pltpu.VMEM)] * 3,
        out_specs=pl.BlockSpec(memory_space=pltpu.VMEM),
        compiler_params=pltpu.CompilerParams(vmem_limit_bytes=32 * 1024 * 1024),
        cost_estimate=pl.CostEstimate(
            flops=4 * places * part * high_count * fronts * border_rows,
            bytes_accessed=4 * (update.size + places * part * high_count),
            transcendentals=0,
        ),
    )(update, place[:, None], high[:, None])


def local(
    child_rhs, pivot_inverse, border_factor, front_sizes, border_index, root_rhs, root_inverse
):
    rows = lax.axis_size("row")
    cols = lax.axis_size("col")
    fronts = lax.axis_size("front")
    layer = fronts * cols
    col_id = lax.axis_index("col")
    row_id = lax.axis_index("row")
    front_id = lax.axis_index("front")
    inverse = pivot_inverse[0]
    border = border_factor[0]
    pivot_rows = inverse.shape[0]
    border_rows = border.shape[0]
    root_rows, sources = root_rhs.shape
    near = 4
    part = sources // near // layer
    halves = 2
    low_count = rows * halves
    high_count = root_rows // halves

    far = rows // near
    block = sources // rows
    step = 1 - 2 * lax.rem(front_id, 2)

    def shift(value, distance, mirrored=True):
        pairs = []
        for front in range(fronts):
            by = -distance if mirrored and front % 2 else distance
            pairs += [(front * rows + z, front * rows + (z + by) % rows) for z in range(rows)]
        return lax.ppermute(value, ("front", "row"), pairs)

    def group_at(offset):
        return lax.rem(row_id + offset + near, near)

    index = []
    for offset in (0, step, -step, 2 * step):
        start = lax.rem(row_id + offset + rows, rows) * border_rows
        live = start + jnp.arange(border_rows, dtype=jnp.int32) < front_sizes[0, 1]
        piece = lax.dynamic_slice_in_dim(border_index[0], start, border_rows)
        index.append(jnp.where(live, piece, -1))
    index = jnp.concatenate(index)

    rhs = child_rhs[0].reshape(-1, far, near, block).transpose(2, 0, 1, 3)
    rhs = rhs.reshape(near, -1, far * block)
    rhs = jnp.stack(
        [
            lax.dynamic_index_in_dim(rhs, group_at(offset), 0, keepdims=False)
            for offset in (2, step, -step, 0)
        ]
    )
    border_above = shift(border, -1)
    border_below = shift(border, 1)
    rhs = lax.all_gather(rhs, "col", axis=1, tiled=True)

    def pivot_product(which):
        return contract(rhs[which], inverse, (0,), (1,))

    from_two = shift(pivot_product(0), -1)
    from_below = shift(pivot_product(1), 1)
    from_two, border_above, border_below = lax.optimization_barrier(
        (from_two, border_above, border_below)
    )
    from_above = shift(pivot_product(2) + from_two, -1)
    near_sum = pivot_product(3) + from_below + from_above
    near_sum = near_sum.reshape(far, block, pivot_rows)
    far_id = lax.div(row_id, near)

    def far_block(offset):
        return lax.dynamic_index_in_dim(near_sum, lax.rem(far_id + offset, far), 0, keepdims=False)

    own = far_block(0)
    sent = [far_block(offset) for offset in range(1, far)]
    *sent, index, border_sent = lax.optimization_barrier((*sent, index, border_above))
    sent = [shift(value, near * (1 + hop), False) for hop, value in enumerate(sent)]
    border_two = shift(border_sent, -1)
    index = lax.all_gather(index, "front", axis=0)
    *sent, index = lax.optimization_barrier((*sent, index))
    for value in sent:
        own = own + value
    pivot_live = col_id * pivot_rows + jnp.arange(pivot_rows, dtype=jnp.int32) < front_sizes[0, 0]
    own = jnp.where(pivot_live[None, :], own, 0.0)

    apart = [[g + near * i for i in range(far)] for g in range(near)]
    solved = lax.all_gather(own, "row", axis_index_groups=apart, axis=0, tiled=True)
    window = (border, border_above, border_below, border_two)
    update = jnp.concatenate([contract(solved, value, (1,), (1,)) for value in window], 1)

    share = front_id * cols + col_id
    per_block = layer // far
    root_share = root_rhs.reshape(root_rows, far, near, per_block, part)
    root_share = lax.dynamic_index_in_dim(root_share, lax.div(share, per_block), 1, keepdims=False)
    root_share = lax.dynamic_index_in_dim(root_share, lax.rem(share, per_block), 2, keepdims=False)
    root_share = root_share.transpose(1, 2, 0)

    def share_of(offset):
        return lax.dynamic_index_in_dim(root_share, group_at(offset), 0, keepdims=False)

    share_rows = root_inverse.shape[0]
    upward = jnp.concatenate([root_inverse, share_of(-1), share_of(-2)])
    downward = jnp.concatenate([root_inverse, share_of(1), share_of(1)])
    update, upward, downward = lax.optimization_barrier((update, upward, downward))
    update = exchange(update.reshape(layer, part, near * border_rows), ("front", "col"))
    upward = shift(upward, -1, False)
    downward = shift(downward, 1, False)

    low = lax.div(jnp.maximum(index, 0), high_count)
    owner = lax.rem(lax.div(low, halves) - lax.rem(row_id, near) + 1 + rows, rows)
    place = jnp.where(index < 0, -1, owner * halves + lax.rem(low, halves))
    high = lax.rem(index, high_count)
    landed = land(update, place, high, fronts, cols, low_count, high_count)
    landed = landed.reshape(far, near * halves * part, high_count)
    landed = lax.all_to_all(landed, "row", 0, 0, axis_index_groups=apart, tiled=True).sum(0)
    landed = landed.reshape(near, halves, part, high_count)

    twice = shift(upward, -1, False)
    shares = jnp.stack(
        [
            downward[share_rows : share_rows + part],
            share_of(0),
            upward[share_rows : share_rows + part],
            twice[share_rows + part :],
        ]
    )
    residual = shares.reshape(near, part, halves, high_count).transpose(0, 2, 1, 3) - landed
    residual = exchange(
        jnp.broadcast_to(residual[None], (layer, near, halves, part, high_count)), ("front", "col")
    )
    residual = residual.transpose(1, 0, 3, 2, 4).reshape(near, far * block, root_rows)

    window = (downward[:share_rows], root_inverse, upward[:share_rows], twice[:share_rows])
    root = sum(contract(residual[i], value, (1,), (1,)) for i, value in enumerate(window))
    root = root.reshape(far, block, share_rows)
    root = lax.all_to_all(root, "row", 0, 0, axis_index_groups=apart, tiled=True).sum(0)
    return own.T[None], root.T


def solution(mesh):
    in_specs = (
        P("front", ("row", "col"), None),
        P("front", "col", "row"),
        P("front", "row", "col"),
        P("front", None),
        P("front", None),
        P("row", None),
        P(("front", "col"), "row"),
    )
    out_specs = (P("front", "col", "row"), P(("front", "col"), "row"))
    return jax.shard_map(local, mesh=mesh, in_specs=in_specs, out_specs=out_specs, check_vma=False)
```

```python
import functools

import jax
import jax.numpy as jnp
from jax import lax
from jax.experimental import pallas as pl
from jax.experimental.pallas import tpu as pltpu
from jax.sharding import PartitionSpec as P

HIGH = lax.Precision.HIGH


def contract(left, right, left_dims, right_dims):
    return lax.dot_general(
        left,
        right,
        ((left_dims, right_dims), ((), ())),
        precision=HIGH,
        preferred_element_type=jnp.float32,
    )


def exchange(blocks, axes):
    return lax.all_to_all(blocks, axes, split_axis=0, concat_axis=0, tiled=True)


def land_kernel(fronts, cols, update_ref, place_ref, high_ref, out_ref):
    part, border_rows = update_ref.shape[1:]
    out_rows, high_count = out_ref.shape
    places = out_rows // part
    repeats = max(1, 8 // part)
    shape = (places // repeats, repeats * part, border_rows)
    place_iota = lax.broadcasted_iota(jnp.int32, shape, 0) * repeats
    place_iota = place_iota + lax.broadcasted_iota(jnp.int32, shape, 1) // part
    high_iota = lax.broadcasted_iota(jnp.int32, (high_count, border_rows), 0)
    total = None
    for front in range(fronts):
        value = update_ref[front * cols]
        for col in range(1, cols):
            value = value + update_ref[front * cols + col]
        value = jnp.concatenate([value] * repeats, 0)
        coarse = value.astype(jnp.bfloat16).astype(jnp.float32)
        at_high = jnp.where(high_iota == high_ref[front], 1.0, 0.0).astype(jnp.bfloat16)
        at_place = place_iota == place_ref[front][None]
        pieces = []
        for piece in (coarse, value - coarse):
            spread = jnp.where(at_place, piece[None], 0.0)
            pieces.append(spread.reshape(out_rows, border_rows).astype(jnp.bfloat16))
        landed = lax.dot_general(
            jnp.concatenate(pieces, 0),
            at_high,
            (((1,), (1,)), ((), ())),
            preferred_element_type=jnp.float32,
        )
        landed = landed[:out_rows] + landed[out_rows:]
        total = landed if total is None else total + landed
    out_ref[...] = total


def land(update, place, high, fronts, cols, places, high_count):
    part, border_rows = update.shape[1:]
    return pl.pallas_call(
        functools.partial(land_kernel, fronts, cols),
        out_shape=jax.ShapeDtypeStruct((places * part, high_count), jnp.float32),
        in_specs=[pl.BlockSpec(memory_space=pltpu.VMEM)] * 3,
        out_specs=pl.BlockSpec(memory_space=pltpu.VMEM),
        compiler_params=pltpu.CompilerParams(vmem_limit_bytes=32 * 1024 * 1024),
        cost_estimate=pl.CostEstimate(
            flops=4 * places * part * high_count * fronts * border_rows,
            bytes_accessed=4 * (update.size + places * part * high_count),
            transcendentals=0,
        ),
    )(update, place[:, None], high[:, None])


def local(
    child_rhs, pivot_inverse, border_factor, front_sizes, border_index, root_rhs, root_inverse
):
    rows = lax.axis_size("row")
    cols = lax.axis_size("col")
    fronts = lax.axis_size("front")
    layer = fronts * cols
    col_id = lax.axis_index("col")
    row_id = lax.axis_index("row")
    front_id = lax.axis_index("front")
    inverse = pivot_inverse[0]
    border = border_factor[0]
    pivot_rows = inverse.shape[0]
    border_rows = border.shape[0]
    root_rows, sources = root_rhs.shape
    near = 4
    part = sources // near // layer
    halves = 2
    low_count = rows * halves
    high_count = root_rows // halves

    far = rows // near
    block = sources // rows
    step = 1 - 2 * lax.rem(front_id, 2)

    def shift(value, distance, mirrored=True):
        pairs = []
        for front in range(fronts):
            by = -distance if mirrored and front % 2 else distance
            pairs += [(front * rows + z, front * rows + (z + by) % rows) for z in range(rows)]
        return lax.ppermute(value, ("front", "row"), pairs)

    def group_at(offset):
        return lax.rem(row_id + offset + near, near)

    index = []
    for offset in (0, step, -step, 2 * step):
        start = lax.rem(row_id + offset + rows, rows) * border_rows
        live = start + jnp.arange(border_rows, dtype=jnp.int32) < front_sizes[0, 1]
        piece = lax.dynamic_slice_in_dim(border_index[0], start, border_rows)
        index.append(jnp.where(live, piece, -1))
    index = jnp.concatenate(index)

    rhs = child_rhs[0].reshape(-1, far, near, block).transpose(2, 0, 1, 3)
    rhs = rhs.reshape(near, -1, far * block)
    rhs = jnp.stack(
        [
            lax.dynamic_index_in_dim(rhs, group_at(offset), 0, keepdims=False)
            for offset in (2, step, -step, 0)
        ]
    )
    border_above = shift(border, -1)
    border_below = shift(border, 1)
    rhs = lax.all_gather(rhs, "col", axis=1, tiled=True)

    def pivot_product(which):
        return contract(rhs[which], inverse, (0,), (1,))

    from_two = shift(pivot_product(0), -1)
    from_below = shift(pivot_product(1), 1)
    from_two, border_above, border_below = lax.optimization_barrier(
        (from_two, border_above, border_below)
    )
    above, border_sent = lax.optimization_barrier((pivot_product(2) + from_two, border_above))
    from_above = shift(above, -1)
    border_two = shift(border_sent, -1)
    near_sum = pivot_product(3) + from_below + from_above
    near_sum = near_sum.reshape(far, block, pivot_rows)
    far_id = lax.div(row_id, near)

    def far_block(offset):
        return lax.dynamic_index_in_dim(near_sum, lax.rem(far_id + offset, far), 0, keepdims=False)

    order = sorted(range(1, far), key=lambda offset: -min(offset, far - offset))
    own = far_block(0)
    sent = [far_block(offset) for offset in order]
    *sent, index = lax.optimization_barrier((*sent, index))
    sent = [shift(value, near * offset, False) for value, offset in zip(sent, order)]
    index = lax.all_gather(index, "front", axis=0)
    *sent, index, border_two = lax.optimization_barrier((*sent, index, border_two))
    for value in sent:
        own = own + value
    pivot_live = col_id * pivot_rows + jnp.arange(pivot_rows, dtype=jnp.int32) < front_sizes[0, 0]
    own = jnp.where(pivot_live[None, :], own, 0.0)

    apart = [[g + near * i for i in range(far)] for g in range(near)]
    solved = lax.all_gather(own, "row", axis_index_groups=apart, axis=0, tiled=True)
    window = (border, border_above, border_below, border_two)
    update = jnp.concatenate([contract(solved, value, (1,), (1,)) for value in window], 1)

    share = front_id * cols + col_id
    per_block = layer // far
    root_share = root_rhs.reshape(root_rows, far, near, per_block, part)
    root_share = lax.dynamic_index_in_dim(root_share, lax.div(share, per_block), 1, keepdims=False)
    root_share = lax.dynamic_index_in_dim(root_share, lax.rem(share, per_block), 2, keepdims=False)
    root_share = root_share.transpose(1, 2, 0)

    def share_of(offset):
        return lax.dynamic_index_in_dim(root_share, group_at(offset), 0, keepdims=False)

    share_rows = root_inverse.shape[0]
    upward = jnp.concatenate([root_inverse, share_of(-1), share_of(-2)])
    downward = jnp.concatenate([root_inverse, share_of(1), share_of(1)])
    update, upward, downward = lax.optimization_barrier((update, upward, downward))
    update = exchange(update.reshape(layer, part, near * border_rows), ("front", "col"))
    upward = shift(upward, -1, False)
    downward = shift(downward, 1, False)

    low = lax.div(jnp.maximum(index, 0), high_count)
    owner = lax.rem(lax.div(low, halves) - lax.rem(row_id, near) + 1 + rows, rows)
    place = jnp.where(index < 0, -1, owner * halves + lax.rem(low, halves))
    high = lax.rem(index, high_count)
    landed = land(update, place, high, fronts, cols, low_count, high_count)
    landed = landed.reshape(far, near * halves * part, high_count)
    landed = lax.all_to_all(landed, "row", 0, 0, axis_index_groups=apart, tiled=True).sum(0)
    landed = landed.reshape(near, halves, part, high_count)

    twice = shift(upward, -1, False)
    shares = jnp.stack(
        [
            downward[share_rows : share_rows + part],
            share_of(0),
            upward[share_rows : share_rows + part],
            twice[share_rows + part :],
        ]
    )
    residual = shares.reshape(near, part, halves, high_count).transpose(0, 2, 1, 3) - landed
    residual = exchange(
        jnp.broadcast_to(residual[None], (layer, near, halves, part, high_count)), ("front", "col")
    )
    residual = residual.transpose(1, 0, 3, 2, 4).reshape(near, far * block, root_rows)

    window = (downward[:share_rows], root_inverse, upward[:share_rows], twice[:share_rows])
    root = sum(contract(residual[i], value, (1,), (1,)) for i, value in enumerate(window))
    root = root.reshape(far, block, share_rows)
    root = lax.all_to_all(root, "row", 0, 0, axis_index_groups=apart, tiled=True).sum(0)
    return own.T[None], root.T


def solution(mesh):
    in_specs = (
        P("front", ("row", "col"), None),
        P("front", "col", "row"),
        P("front", "row", "col"),
        P("front", None),
        P("front", None),
        P("row", None),
        P(("front", "col"), "row"),
    )
    out_specs = (P("front", "col", "row"), P(("front", "col"), "row"))
    return jax.shard_map(local, mesh=mesh, in_specs=in_specs, out_specs=out_specs, check_vma=False)
```

```python
import functools

import jax
import jax.numpy as jnp
from jax import lax
from jax.experimental import pallas as pl
from jax.experimental.pallas import tpu as pltpu
from jax.sharding import PartitionSpec as P

HIGH = lax.Precision.HIGH


def contract(left, right, left_dims, right_dims):
    return lax.dot_general(
        left,
        right,
        ((left_dims, right_dims), ((), ())),
        precision=HIGH,
        preferred_element_type=jnp.float32,
    )


def exchange(blocks, axes):
    return lax.all_to_all(blocks, axes, split_axis=0, concat_axis=0, tiled=True)


def land_kernel(fronts, cols, border_rows, update_ref, out_ref):
    part = update_ref.shape[1]
    out_rows, high_count = out_ref.shape
    places = out_rows // part
    repeats = max(1, 8 // part)
    shape = (places // repeats, repeats * part, border_rows)
    place_iota = lax.broadcasted_iota(jnp.int32, shape, 0) * repeats
    place_iota = place_iota + lax.broadcasted_iota(jnp.int32, shape, 1) // part
    high_iota = lax.broadcasted_iota(jnp.int32, (high_count, border_rows), 0)
    total = None
    for front in range(fronts):
        value = update_ref[front * cols][:, :border_rows]
        for col in range(1, cols):
            value = value + update_ref[front * cols + col][:, :border_rows]
        codes = update_ref[front * cols][:, border_rows:]
        codes = jnp.concatenate([codes[row : row + 1] for row in range(part)], 1).astype(jnp.int32)
        place = jnp.where(codes < 0, -1, codes // high_count)
        high = codes % high_count
        value = jnp.concatenate([value] * repeats, 0)
        coarse = value.astype(jnp.bfloat16).astype(jnp.float32)
        at_high = jnp.where(high_iota == high, 1.0, 0.0).astype(jnp.bfloat16)
        at_place = place_iota == place[None]
        pieces = []
        for piece in (coarse, value - coarse):
            spread = jnp.where(at_place, piece[None], 0.0)
            pieces.append(spread.reshape(out_rows, border_rows).astype(jnp.bfloat16))
        landed = lax.dot_general(
            jnp.concatenate(pieces, 0),
            at_high,
            (((1,), (1,)), ((), ())),
            preferred_element_type=jnp.float32,
        )
        landed = landed[:out_rows] + landed[out_rows:]
        total = landed if total is None else total + landed
    out_ref[...] = total


def land(update, border_rows, fronts, cols, places, high_count):
    part = update.shape[1]
    return pl.pallas_call(
        functools.partial(land_kernel, fronts, cols, border_rows),
        out_shape=jax.ShapeDtypeStruct((places * part, high_count), jnp.float32),
        in_specs=[pl.BlockSpec(memory_space=pltpu.VMEM)],
        out_specs=pl.BlockSpec(memory_space=pltpu.VMEM),
        compiler_params=pltpu.CompilerParams(vmem_limit_bytes=32 * 1024 * 1024),
        cost_estimate=pl.CostEstimate(
            flops=4 * places * part * high_count * fronts * border_rows,
            bytes_accessed=4 * (update.size + places * part * high_count),
            transcendentals=0,
        ),
    )(update)


def local(
    child_rhs, pivot_inverse, border_factor, front_sizes, border_index, root_rhs, root_inverse
):
    rows = lax.axis_size("row")
    cols = lax.axis_size("col")
    fronts = lax.axis_size("front")
    layer = fronts * cols
    col_id = lax.axis_index("col")
    row_id = lax.axis_index("row")
    front_id = lax.axis_index("front")
    inverse = pivot_inverse[0]
    border = border_factor[0]
    pivot_rows = inverse.shape[0]
    border_rows = border.shape[0]
    root_rows, sources = root_rhs.shape
    near = 4
    part = sources // near // layer
    halves = 2
    low_count = rows * halves
    high_count = root_rows // halves

    far = rows // near
    block = sources // rows
    step = 1 - 2 * lax.rem(front_id, 2)

    def shift(value, distance, mirrored=True):
        pairs = []
        for front in range(fronts):
            by = -distance if mirrored and front % 2 else distance
            pairs += [(front * rows + z, front * rows + (z + by) % rows) for z in range(rows)]
        return lax.ppermute(value, ("front", "row"), pairs)

    def group_at(offset):
        return lax.rem(row_id + offset + near, near)

    index = []
    for offset in (0, step, -step, 2 * step):
        start = lax.rem(row_id + offset + rows, rows) * border_rows
        live = start + jnp.arange(border_rows, dtype=jnp.int32) < front_sizes[0, 1]
        piece = lax.dynamic_slice_in_dim(border_index[0], start, border_rows)
        index.append(jnp.where(live, piece, -1))
    index = jnp.concatenate(index)
    low = lax.div(jnp.maximum(index, 0), high_count)
    owner = lax.rem(lax.div(low, halves) - lax.rem(row_id, near) + 1 + rows, rows)
    code = (owner * halves + lax.rem(low, halves)) * high_count + lax.rem(index, high_count)
    code = jnp.where(index < 0, -1, code).astype(jnp.float32)
    code = jnp.tile(code.reshape(part, -1), (layer, 1))

    rhs = child_rhs[0].reshape(-1, far, near, block).transpose(2, 0, 1, 3)
    rhs = rhs.reshape(near, -1, far * block)
    rhs = jnp.stack(
        [
            lax.dynamic_index_in_dim(rhs, group_at(offset), 0, keepdims=False)
            for offset in (2, step, -step, 0)
        ]
    )
    border_above = shift(border, -1)
    border_below = shift(border, 1)
    rhs = lax.all_gather(rhs, "col", axis=1, tiled=True)

    def pivot_product(which):
        return contract(rhs[which], inverse, (0,), (1,))

    from_two = shift(pivot_product(0), -1)
    from_below = shift(pivot_product(1), 1)
    from_two, border_above, border_below = lax.optimization_barrier(
        (from_two, border_above, border_below)
    )
    above, border_sent = lax.optimization_barrier((pivot_product(2) + from_two, border_above))
    from_above = shift(above, -1)
    border_two = shift(border_sent, -1)
    near_sum = pivot_product(3) + from_below + from_above
    near_sum = near_sum.reshape(far, block, pivot_rows)
    far_id = lax.div(row_id, near)

    def far_block(offset):
        return lax.dynamic_index_in_dim(near_sum, lax.rem(far_id + offset, far), 0, keepdims=False)

    own = far_block(0)
    sent = []
    for offset in sorted(range(1, far), key=lambda offset: -min(offset, far - offset)):
        sent.append(shift(far_block(offset), near * offset, False))
    *sent, border_two = lax.optimization_barrier((*sent, border_two))
    for value in sent:
        own = own + value
    pivot_live = col_id * pivot_rows + jnp.arange(pivot_rows, dtype=jnp.int32) < front_sizes[0, 0]
    own = jnp.where(pivot_live[None, :], own, 0.0)

    apart = [[g + near * i for i in range(far)] for g in range(near)]
    solved = lax.all_gather(own, "row", axis_index_groups=apart, axis=0, tiled=True)
    window = (border, border_above, border_below, border_two)
    update = [contract(solved, value, (1,), (1,)) for value in window]
    update = jnp.concatenate([*update, code], 1)

    share = front_id * cols + col_id
    per_block = layer // far
    root_share = root_rhs.reshape(root_rows, far, near, per_block, part)
    root_share = lax.dynamic_index_in_dim(root_share, lax.div(share, per_block), 1, keepdims=False)
    root_share = lax.dynamic_index_in_dim(root_share, lax.rem(share, per_block), 2, keepdims=False)
    root_share = root_share.transpose(1, 2, 0)

    def share_of(offset):
        return lax.dynamic_index_in_dim(root_share, group_at(offset), 0, keepdims=False)

    share_rows = root_inverse.shape[0]
    upward = jnp.concatenate([root_inverse, share_of(-1), share_of(-2)])
    downward = jnp.concatenate([root_inverse, share_of(1), share_of(1)])
    update, upward, downward = lax.optimization_barrier((update, upward, downward))
    update = exchange(update.reshape(layer, part, -1), ("front", "col"))
    upward = shift(upward, -1, False)
    downward = shift(downward, 1, False)

    landed = land(update, near * border_rows, fronts, cols, low_count, high_count)
    landed = landed.reshape(far, near * halves * part, high_count)
    landed = lax.all_to_all(landed, "row", 0, 0, axis_index_groups=apart, tiled=True).sum(0)
    landed = landed.reshape(near, halves, part, high_count)

    twice = shift(upward, -1, False)
    shares = jnp.stack(
        [
            downward[share_rows : share_rows + part],
            share_of(0),
            upward[share_rows : share_rows + part],
            twice[share_rows + part :],
        ]
    )
    residual = shares.reshape(near, part, halves, high_count).transpose(0, 2, 1, 3) - landed
    residual = exchange(
        jnp.broadcast_to(residual[None], (layer, near, halves, part, high_count)), ("front", "col")
    )
    residual = residual.transpose(1, 0, 3, 2, 4).reshape(near, far * block, root_rows)

    window = (downward[:share_rows], root_inverse, upward[:share_rows], twice[:share_rows])
    root = sum(contract(residual[i], value, (1,), (1,)) for i, value in enumerate(window))
    root = root.reshape(far, block, share_rows)
    root = lax.all_to_all(root, "row", 0, 0, axis_index_groups=apart, tiled=True).sum(0)
    return own.T[None], root.T


def solution(mesh):
    in_specs = (
        P("front", ("row", "col"), None),
        P("front", "col", "row"),
        P("front", "row", "col"),
        P("front", None),
        P("front", None),
        P("row", None),
        P(("front", "col"), "row"),
    )
    out_specs = (P("front", "col", "row"), P(("front", "col"), "row"))
    return jax.shard_map(local, mesh=mesh, in_specs=in_specs, out_specs=out_specs, check_vma=False)
```

```python
import functools

import jax
import jax.numpy as jnp
from jax import lax
from jax.experimental import pallas as pl
from jax.experimental.pallas import tpu as pltpu
from jax.sharding import PartitionSpec as P

HIGH = lax.Precision.HIGH


def contract(left, right, left_dims, right_dims):
    return lax.dot_general(
        left,
        right,
        ((left_dims, right_dims), ((), ())),
        precision=HIGH,
        preferred_element_type=jnp.float32,
    )


def exchange(blocks, axes):
    return lax.all_to_all(blocks, axes, split_axis=0, concat_axis=0, tiled=True)


def land_kernel(fronts, cols, border_rows, update_ref, out_ref):
    part = update_ref.shape[1]
    out_rows, high_count = out_ref.shape
    places = out_rows // part
    repeats = max(1, 8 // part)
    shape = (places // repeats, repeats * part, border_rows)
    place_iota = lax.broadcasted_iota(jnp.int32, shape, 0) * repeats
    place_iota = place_iota + lax.broadcasted_iota(jnp.int32, shape, 1) // part
    high_iota = lax.broadcasted_iota(jnp.int32, (high_count, border_rows), 0)
    total = None
    for front in range(fronts):
        value = update_ref[front * cols][:, :border_rows]
        for col in range(1, cols):
            value = value + update_ref[front * cols + col][:, :border_rows]
        codes = update_ref[front * cols][:, border_rows:]
        codes = jnp.concatenate([codes[row : row + 1] for row in range(part)], 1).astype(jnp.int32)
        place = jnp.where(codes < 0, -1, codes // high_count)
        high = codes % high_count
        value = jnp.concatenate([value] * repeats, 0)
        coarse = value.astype(jnp.bfloat16).astype(jnp.float32)
        at_high = jnp.where(high_iota == high, 1.0, 0.0).astype(jnp.bfloat16)
        at_place = place_iota == place[None]
        pieces = []
        for piece in (coarse, value - coarse):
            spread = jnp.where(at_place, piece[None], 0.0)
            pieces.append(spread.reshape(out_rows, border_rows).astype(jnp.bfloat16))
        landed = lax.dot_general(
            jnp.concatenate(pieces, 0),
            at_high,
            (((1,), (1,)), ((), ())),
            preferred_element_type=jnp.float32,
        )
        landed = landed[:out_rows] + landed[out_rows:]
        total = landed if total is None else total + landed
    out_ref[...] = total


def land(update, border_rows, fronts, cols, places, high_count):
    part = update.shape[1]
    return pl.pallas_call(
        functools.partial(land_kernel, fronts, cols, border_rows),
        out_shape=jax.ShapeDtypeStruct((places * part, high_count), jnp.float32),
        in_specs=[pl.BlockSpec(memory_space=pltpu.VMEM)],
        out_specs=pl.BlockSpec(memory_space=pltpu.VMEM),
        compiler_params=pltpu.CompilerParams(vmem_limit_bytes=32 * 1024 * 1024),
        cost_estimate=pl.CostEstimate(
            flops=4 * places * part * high_count * fronts * border_rows,
            bytes_accessed=4 * (update.size + places * part * high_count),
            transcendentals=0,
        ),
    )(update)


def local(
    child_rhs, pivot_inverse, border_factor, front_sizes, border_index, root_rhs, root_inverse
):
    rows = lax.axis_size("row")
    cols = lax.axis_size("col")
    fronts = lax.axis_size("front")
    layer = fronts * cols
    col_id = lax.axis_index("col")
    row_id = lax.axis_index("row")
    front_id = lax.axis_index("front")
    inverse = pivot_inverse[0]
    border = border_factor[0]
    pivot_rows = inverse.shape[0]
    border_rows = border.shape[0]
    root_rows, sources = root_rhs.shape
    near = 4
    part = sources // near // layer
    halves = 2
    low_count = rows * halves
    high_count = root_rows // halves

    far = rows // near
    block = sources // rows
    step = 1 - 2 * lax.rem(front_id, 2)

    def shift(value, distance, mirrored=True):
        pairs = []
        for front in range(fronts):
            by = -distance if mirrored and front % 2 else distance
            pairs += [(front * rows + z, front * rows + (z + by) % rows) for z in range(rows)]
        return lax.ppermute(value, ("front", "row"), pairs)

    def group_at(offset):
        return lax.rem(row_id + offset + near, near)

    index = []
    for offset in (0, step, -step, 2 * step):
        start = lax.rem(row_id + offset + rows, rows) * border_rows
        live = start + jnp.arange(border_rows, dtype=jnp.int32) < front_sizes[0, 1]
        piece = lax.dynamic_slice_in_dim(border_index[0], start, border_rows)
        index.append(jnp.where(live, piece, -1))
    index = jnp.concatenate(index)
    low = lax.div(jnp.maximum(index, 0), high_count)
    owner = lax.rem(lax.div(low, halves) - lax.rem(row_id, near) + 1 + rows, rows)
    code = (owner * halves + lax.rem(low, halves)) * high_count + lax.rem(index, high_count)
    code = jnp.where(index < 0, -1, code).astype(jnp.float32)
    code = jnp.tile(code.reshape(part, -1), (layer, 1))

    rhs = child_rhs[0].reshape(-1, far, near, block).transpose(2, 0, 1, 3)
    rhs = rhs.reshape(near, -1, far * block)
    rhs = jnp.stack(
        [
            lax.dynamic_index_in_dim(rhs, group_at(offset), 0, keepdims=False)
            for offset in (2, step, -step, 0)
        ]
    )
    border_above = shift(border, -1)
    border_below = shift(border, 1)
    rhs = lax.all_gather(rhs, "col", axis=1, tiled=True)

    def pivot_product(which):
        return contract(rhs[which], inverse, (0,), (1,))

    from_two = shift(pivot_product(0), -1)
    from_below = shift(pivot_product(1), 1)
    from_two, border_above, border_below = lax.optimization_barrier(
        (from_two, border_above, border_below)
    )
    above, border_sent = lax.optimization_barrier((pivot_product(2) + from_two, border_above))
    from_above = shift(above, -1)
    border_two = shift(border_sent, -1)
    near_sum = pivot_product(3) + from_below + from_above
    near_sum = near_sum.reshape(far, block, pivot_rows)
    far_id = lax.div(row_id, near)

    def far_block(offset):
        return lax.dynamic_index_in_dim(near_sum, lax.rem(far_id + offset, far), 0, keepdims=False)

    share = front_id * cols + col_id
    per_block = layer // far
    root_share = root_rhs.reshape(root_rows, far, near, per_block, part)
    root_share = lax.dynamic_index_in_dim(root_share, lax.div(share, per_block), 1, keepdims=False)
    root_share = lax.dynamic_index_in_dim(root_share, lax.rem(share, per_block), 2, keepdims=False)
    root_share = root_share.transpose(1, 2, 0)

    def share_of(offset):
        return lax.dynamic_index_in_dim(root_share, group_at(offset), 0, keepdims=False)

    own = far_block(0)
    sent = []
    for offset in sorted(range(1, far), key=lambda offset: -min(offset, far - offset)):
        sent.append(shift(far_block(offset), near * offset, False))
    share_two = shift(share_of(-2), -2, False)
    *sent, border_two, share_two = lax.optimization_barrier((*sent, border_two, share_two))
    for value in sent:
        own = own + value
    pivot_live = col_id * pivot_rows + jnp.arange(pivot_rows, dtype=jnp.int32) < front_sizes[0, 0]
    own = jnp.where(pivot_live[None, :], own, 0.0)

    apart = [[g + near * i for i in range(far)] for g in range(near)]
    solved = lax.all_gather(own, "row", axis_index_groups=apart, axis=0, tiled=True)
    window = (border, border_above, border_below, border_two)
    update = [contract(solved, value, (1,), (1,)) for value in window]
    update = jnp.concatenate([*update, code], 1)

    share_rows = root_inverse.shape[0]
    upward = jnp.concatenate([root_inverse, share_of(-1), share_of(-1)])
    downward = jnp.concatenate([root_inverse, share_of(1), share_of(1)])
    update, upward, downward = lax.optimization_barrier((update, upward, downward))
    update = exchange(update.reshape(layer, part, -1), ("front", "col"))
    upward = shift(upward, -1, False)
    downward = shift(downward, 1, False)

    landed = land(update, near * border_rows, fronts, cols, low_count, high_count)
    landed = landed.reshape(far, near * halves * part, high_count)
    landed = lax.all_to_all(landed, "row", 0, 0, axis_index_groups=apart, tiled=True).sum(0)
    landed = landed.reshape(near, halves, part, high_count)

    shares = jnp.stack(
        [
            downward[share_rows : share_rows + part],
            share_of(0),
            upward[share_rows : share_rows + part],
            share_two,
        ]
    )
    residual = shares.reshape(near, part, halves, high_count).transpose(0, 2, 1, 3) - landed
    residual, upward = lax.optimization_barrier((residual, upward))
    twice = shift(upward[:share_rows], -1, False)
    residual = exchange(
        jnp.broadcast_to(residual[None], (layer, near, halves, part, high_count)), ("front", "col")
    )
    residual = residual.transpose(1, 0, 3, 2, 4).reshape(near, far * block, root_rows)

    window = (downward[:share_rows], root_inverse, upward[:share_rows], twice)
    root = sum(contract(residual[i], value, (1,), (1,)) for i, value in enumerate(window))
    root = root.reshape(far, block, share_rows)
    root = lax.all_to_all(root, "row", 0, 0, axis_index_groups=apart, tiled=True).sum(0)
    return own.T[None], root.T


def solution(mesh):
    in_specs = (
        P("front", ("row", "col"), None),
        P("front", "col", "row"),
        P("front", "row", "col"),
        P("front", None),
        P("front", None),
        P("row", None),
        P(("front", "col"), "row"),
    )
    out_specs = (P("front", "col", "row"), P(("front", "col"), "row"))
    return jax.shard_map(local, mesh=mesh, in_specs=in_specs, out_specs=out_specs, check_vma=False)
```

```python
import functools

import jax
import jax.numpy as jnp
from jax import lax
from jax.experimental import pallas as pl
from jax.experimental.pallas import tpu as pltpu
from jax.sharding import PartitionSpec as P

HIGH = lax.Precision.HIGH


def contract(left, right, left_dims, right_dims):
    return lax.dot_general(
        left,
        right,
        ((left_dims, right_dims), ((), ())),
        precision=HIGH,
        preferred_element_type=jnp.float32,
    )


def exchange(blocks, axes):
    return lax.all_to_all(blocks, axes, split_axis=0, concat_axis=0, tiled=True)


def land_kernel(fronts, cols, border_rows, update_ref, out_ref):
    part = update_ref.shape[1]
    out_rows, high_count = out_ref.shape
    places = out_rows // part
    repeats = max(1, 8 // part)
    shape = (places // repeats, repeats * part, border_rows)
    place_iota = lax.broadcasted_iota(jnp.int32, shape, 0) * repeats
    place_iota = place_iota + lax.broadcasted_iota(jnp.int32, shape, 1) // part
    high_iota = lax.broadcasted_iota(jnp.int32, (high_count, border_rows), 0)
    total = None
    for front in range(fronts):
        value = update_ref[front * cols][:, :border_rows]
        for col in range(1, cols):
            value = value + update_ref[front * cols + col][:, :border_rows]
        codes = update_ref[front * cols][:, border_rows:]
        codes = jnp.concatenate([codes[row : row + 1] for row in range(part)], 1).astype(jnp.int32)
        place = jnp.where(codes < 0, -1, codes // high_count)
        high = codes % high_count
        value = jnp.concatenate([value] * repeats, 0)
        coarse = value.astype(jnp.bfloat16).astype(jnp.float32)
        at_high = jnp.where(high_iota == high, 1.0, 0.0).astype(jnp.bfloat16)
        at_place = place_iota == place[None]
        pieces = []
        for piece in (coarse, value - coarse):
            spread = jnp.where(at_place, piece[None], 0.0)
            pieces.append(spread.reshape(out_rows, border_rows).astype(jnp.bfloat16))
        landed = lax.dot_general(
            jnp.concatenate(pieces, 0),
            at_high,
            (((1,), (1,)), ((), ())),
            preferred_element_type=jnp.float32,
        )
        landed = landed[:out_rows] + landed[out_rows:]
        total = landed if total is None else total + landed
    out_ref[...] = total


def land(update, border_rows, fronts, cols, places, high_count):
    part = update.shape[1]
    return pl.pallas_call(
        functools.partial(land_kernel, fronts, cols, border_rows),
        out_shape=jax.ShapeDtypeStruct((places * part, high_count), jnp.float32),
        in_specs=[pl.BlockSpec(memory_space=pltpu.VMEM)],
        out_specs=pl.BlockSpec(memory_space=pltpu.VMEM),
        compiler_params=pltpu.CompilerParams(vmem_limit_bytes=32 * 1024 * 1024),
        cost_estimate=pl.CostEstimate(
            flops=4 * places * part * high_count * fronts * border_rows,
            bytes_accessed=4 * (update.size + places * part * high_count),
            transcendentals=0,
        ),
    )(update)


def local(
    child_rhs, pivot_inverse, border_factor, front_sizes, border_index, root_rhs, root_inverse
):
    rows = lax.axis_size("row")
    cols = lax.axis_size("col")
    fronts = lax.axis_size("front")
    layer = fronts * cols
    col_id = lax.axis_index("col")
    row_id = lax.axis_index("row")
    front_id = lax.axis_index("front")
    inverse = pivot_inverse[0]
    border = border_factor[0]
    pivot_rows = inverse.shape[0]
    border_rows = border.shape[0]
    root_rows, sources = root_rhs.shape
    near = 4
    part = sources // near // layer
    halves = 2
    low_count = rows * halves
    high_count = root_rows // halves

    far = rows // near
    block = sources // rows
    step = 1 - 2 * lax.rem(front_id, 2)

    def shift(value, distance, mirrored=True):
        pairs = []
        for front in range(fronts):
            by = -distance if mirrored and front % 2 else distance
            pairs += [(front * rows + z, front * rows + (z + by) % rows) for z in range(rows)]
        return lax.ppermute(value, ("front", "row"), pairs)

    def group_at(offset):
        return lax.rem(row_id + offset + near, near)

    index = []
    for offset in (0, step, -step, 2 * step):
        start = lax.rem(row_id + offset + rows, rows) * border_rows
        live = start + jnp.arange(border_rows, dtype=jnp.int32) < front_sizes[0, 1]
        piece = lax.dynamic_slice_in_dim(border_index[0], start, border_rows)
        index.append(jnp.where(live, piece, -1))
    index = jnp.concatenate(index)
    low = lax.div(jnp.maximum(index, 0), high_count)
    owner = lax.rem(lax.div(low, halves) - lax.rem(row_id, near) + 1 + rows, rows)
    code = (owner * halves + lax.rem(low, halves)) * high_count + lax.rem(index, high_count)
    code = jnp.where(index < 0, -1, code).astype(jnp.float32)
    code = jnp.tile(code.reshape(part, -1), (layer, 1))

    rhs = child_rhs[0].reshape(-1, far, near, block).transpose(2, 0, 1, 3)
    rhs = rhs.reshape(near, -1, far * block)
    rhs = jnp.stack(
        [
            lax.dynamic_index_in_dim(rhs, group_at(offset), 0, keepdims=False)
            for offset in (2, step, -step, 0)
        ]
    )
    border_above = shift(border, -1)
    border_below = shift(border, 1)
    rhs = lax.all_gather(rhs, "col", axis=1, tiled=True)

    def pivot_product(which):
        return contract(rhs[which], inverse, (0,), (1,))

    from_two = shift(pivot_product(0), -1)
    from_below = shift(pivot_product(1), 1)
    from_two, border_above, border_below = lax.optimization_barrier(
        (from_two, border_above, border_below)
    )
    above, border_sent = lax.optimization_barrier((pivot_product(2) + from_two, border_above))
    from_above = shift(above, -1)
    border_two = shift(border_sent, -1)
    near_sum = pivot_product(3) + from_below + from_above
    near_sum = near_sum.reshape(far, block, pivot_rows)
    far_id = lax.div(row_id, near)

    def far_block(offset):
        return lax.dynamic_index_in_dim(near_sum, lax.rem(far_id + offset, far), 0, keepdims=False)

    own = far_block(0)
    sent = []
    for offset in sorted(range(1, far), key=lambda offset: -min(offset, far - offset)):
        sent.append(shift(far_block(offset), near * offset, False))
    *sent, border_two = lax.optimization_barrier((*sent, border_two))
    for value in sent:
        own = own + value
    pivot_live = col_id * pivot_rows + jnp.arange(pivot_rows, dtype=jnp.int32) < front_sizes[0, 0]
    own = jnp.where(pivot_live[None, :], own, 0.0)

    apart = [[g + near * i for i in range(far)] for g in range(near)]
    solved = lax.all_gather(own, "row", axis_index_groups=apart, axis=0, tiled=True)
    window = (border, border_above, border_below, border_two)
    update = [contract(solved, value, (1,), (1,)) for value in window]
    update = jnp.concatenate([*update, code], 1)

    share = front_id * cols + col_id
    per_block = layer // far
    root_share = root_rhs.reshape(root_rows, far, near, per_block, part)
    root_share = lax.dynamic_index_in_dim(root_share, lax.div(share, per_block), 1, keepdims=False)
    root_share = lax.dynamic_index_in_dim(root_share, lax.rem(share, per_block), 2, keepdims=False)
    root_share = root_share.transpose(1, 2, 0)

    def share_of(offset):
        return lax.dynamic_index_in_dim(root_share, group_at(offset), 0, keepdims=False)

    share_rows = root_inverse.shape[0]
    upward = jnp.concatenate([root_inverse, share_of(-1), share_of(-2)])
    downward = jnp.concatenate([root_inverse, share_of(1), share_of(1)])
    update, upward, downward = lax.optimization_barrier((update, upward, downward))
    update = exchange(update.reshape(layer, part, -1), ("front", "col"))
    upward = shift(upward, -1, False)
    downward = shift(downward, 1, False)

    landed = land(update, near * border_rows, fronts, cols, low_count, high_count)
    landed, upward = lax.optimization_barrier((landed, upward))
    twice = shift(upward, -1, False)
    landed = landed.reshape(far, near * halves * part, high_count)
    landed = lax.all_to_all(landed, "row", 0, 0, axis_index_groups=apart, tiled=True).sum(0)
    landed = landed.reshape(near, halves, part, high_count)

    shares = jnp.stack(
        [
            downward[share_rows : share_rows + part],
            share_of(0),
            upward[share_rows : share_rows + part],
            twice[share_rows + part :],
        ]
    )
    residual = shares.reshape(near, part, halves, high_count).transpose(0, 2, 1, 3) - landed
    residual = exchange(
        jnp.broadcast_to(residual[None], (layer, near, halves, part, high_count)), ("front", "col")
    )
    residual = residual.transpose(1, 0, 3, 2, 4).reshape(near, far * block, root_rows)

    window = (downward[:share_rows], root_inverse, upward[:share_rows], twice[:share_rows])
    root = sum(contract(residual[i], value, (1,), (1,)) for i, value in enumerate(window))
    root = root.reshape(far, block, share_rows)
    root = lax.all_to_all(root, "row", 0, 0, axis_index_groups=apart, tiled=True).sum(0)
    return own.T[None], root.T


def solution(mesh):
    in_specs = (
        P("front", ("row", "col"), None),
        P("front", "col", "row"),
        P("front", "row", "col"),
        P("front", None),
        P("front", None),
        P("row", None),
        P(("front", "col"), "row"),
    )
    out_specs = (P("front", "col", "row"), P(("front", "col"), "row"))
    return jax.shard_map(local, mesh=mesh, in_specs=in_specs, out_specs=out_specs, check_vma=False)
```

```python
import functools

import jax
import jax.numpy as jnp
from jax import lax
from jax.experimental import pallas as pl
from jax.experimental.pallas import tpu as pltpu
from jax.sharding import PartitionSpec as P

HIGH = lax.Precision.HIGH


def contract(left, right, left_dims, right_dims):
    return lax.dot_general(
        left,
        right,
        ((left_dims, right_dims), ((), ())),
        precision=HIGH,
        preferred_element_type=jnp.float32,
    )


def exchange(blocks, axes):
    return lax.all_to_all(blocks, axes, split_axis=0, concat_axis=0, tiled=True)


def land_kernel(fronts, cols, update_ref, place_ref, high_ref, out_ref):
    part, border_rows = update_ref.shape[1:]
    out_rows, high_count = out_ref.shape
    places = out_rows // part
    repeats = max(1, 8 // part)
    shape = (places // repeats, repeats * part, border_rows)
    place_iota = lax.broadcasted_iota(jnp.int32, shape, 0) * repeats
    place_iota = place_iota + lax.broadcasted_iota(jnp.int32, shape, 1) // part
    high_iota = lax.broadcasted_iota(jnp.int32, (high_count, border_rows), 0)
    total = None
    for front in range(fronts):
        value = update_ref[front * cols]
        for col in range(1, cols):
            value = value + update_ref[front * cols + col]
        value = jnp.concatenate([value] * repeats, 0)
        coarse = value.astype(jnp.bfloat16).astype(jnp.float32)
        at_high = jnp.where(high_iota == high_ref[front], 1.0, 0.0).astype(jnp.bfloat16)
        at_place = place_iota == place_ref[front][None]
        pieces = []
        for piece in (coarse, value - coarse):
            spread = jnp.where(at_place, piece[None], 0.0)
            pieces.append(spread.reshape(out_rows, border_rows).astype(jnp.bfloat16))
        landed = lax.dot_general(
            jnp.concatenate(pieces, 0),
            at_high,
            (((1,), (1,)), ((), ())),
            preferred_element_type=jnp.float32,
        )
        landed = landed[:out_rows] + landed[out_rows:]
        total = landed if total is None else total + landed
    out_ref[...] = total


def land(update, place, high, fronts, cols, places, high_count):
    part, border_rows = update.shape[1:]
    return pl.pallas_call(
        functools.partial(land_kernel, fronts, cols),
        out_shape=jax.ShapeDtypeStruct((places * part, high_count), jnp.float32),
        in_specs=[pl.BlockSpec(memory_space=pltpu.VMEM)] * 3,
        out_specs=pl.BlockSpec(memory_space=pltpu.VMEM),
        compiler_params=pltpu.CompilerParams(vmem_limit_bytes=32 * 1024 * 1024),
        cost_estimate=pl.CostEstimate(
            flops=4 * places * part * high_count * fronts * border_rows,
            bytes_accessed=4 * (update.size + places * part * high_count),
            transcendentals=0,
        ),
    )(update, place[:, None], high[:, None])


def local(
    child_rhs, pivot_inverse, border_factor, front_sizes, border_index, root_rhs, root_inverse
):
    rows = lax.axis_size("row")
    cols = lax.axis_size("col")
    fronts = lax.axis_size("front")
    layer = fronts * cols
    col_id = lax.axis_index("col")
    row_id = lax.axis_index("row")
    front_id = lax.axis_index("front")
    inverse = pivot_inverse[0]
    border = border_factor[0]
    pivot_rows = inverse.shape[0]
    border_rows = border.shape[0]
    root_rows, sources = root_rhs.shape
    near = 4
    part = sources // near // layer
    halves = 2
    low_count = rows * halves
    high_count = root_rows // halves

    far = rows // near
    block = sources // rows
    step = 1 - 2 * lax.rem(front_id, 2)

    def shift(value, distance, mirrored=True):
        pairs = []
        for front in range(fronts):
            by = -distance if mirrored and front % 2 else distance
            pairs += [(front * rows + z, front * rows + (z + by) % rows) for z in range(rows)]
        return lax.ppermute(value, ("front", "row"), pairs)

    def group_at(offset):
        return lax.rem(row_id + offset + near, near)

    index = []
    for offset in (0, step, -step, 2 * step):
        start = lax.rem(row_id + offset + rows, rows) * border_rows
        live = start + jnp.arange(border_rows, dtype=jnp.int32) < front_sizes[0, 1]
        piece = lax.dynamic_slice_in_dim(border_index[0], start, border_rows)
        index.append(jnp.where(live, piece, -1))
    index = jnp.concatenate(index)

    rhs = child_rhs[0].reshape(-1, far, near, block).transpose(2, 0, 1, 3)
    rhs = rhs.reshape(near, -1, far * block)
    rhs = jnp.stack(
        [
            lax.dynamic_index_in_dim(rhs, group_at(offset), 0, keepdims=False)
            for offset in (2, step, -step, 0)
        ]
    )
    border_above = shift(border, -1)
    border_below = shift(border, 1)
    rhs = lax.all_gather(rhs, "col", axis=1, tiled=True)

    def pivot_product(which):
        return contract(rhs[which], inverse, (0,), (1,))

    from_two = shift(pivot_product(0), -1)
    from_below = shift(pivot_product(1), 1)
    from_two, border_above, border_below = lax.optimization_barrier(
        (from_two, border_above, border_below)
    )
    above, border_sent = lax.optimization_barrier((pivot_product(2) + from_two, border_above))
    from_above = shift(above, -1)
    border_two = shift(border_sent, -1)
    near_sum = pivot_product(3) + from_below + from_above
    near_sum = near_sum.reshape(far, block, pivot_rows)
    far_id = lax.div(row_id, near)

    def far_block(offset):
        return lax.dynamic_index_in_dim(near_sum, lax.rem(far_id + offset, far), 0, keepdims=False)

    order = sorted(range(1, far), key=lambda offset: -min(offset, far - offset))
    own = far_block(0)
    sent = [far_block(offset) for offset in order]
    *sent, index = lax.optimization_barrier((*sent, index))
    sent = [shift(value, near * offset, False) for value, offset in zip(sent, order)]
    index = lax.all_gather(index, "front", axis=0)
    *sent, index, border_two = lax.optimization_barrier((*sent, index, border_two))
    for value in sent:
        own = own + value
    pivot_live = col_id * pivot_rows + jnp.arange(pivot_rows, dtype=jnp.int32) < front_sizes[0, 0]
    own = jnp.where(pivot_live[None, :], own, 0.0)

    apart = [[g + near * i for i in range(far)] for g in range(near)]
    solved = lax.all_gather(own, "row", axis_index_groups=apart, axis=0, tiled=True)
    window = (border, border_above, border_below, border_two)
    update = jnp.concatenate([contract(solved, value, (1,), (1,)) for value in window], 1)

    share = front_id * cols + col_id
    per_block = layer // far
    root_share = root_rhs.reshape(root_rows, far, near, per_block, part)
    root_share = lax.dynamic_index_in_dim(root_share, lax.div(share, per_block), 1, keepdims=False)
    root_share = lax.dynamic_index_in_dim(root_share, lax.rem(share, per_block), 2, keepdims=False)
    root_share = root_share.transpose(1, 2, 0)

    def share_of(offset):
        return lax.dynamic_index_in_dim(root_share, group_at(offset), 0, keepdims=False)

    share_rows = root_inverse.shape[0]
    upward = jnp.concatenate([root_inverse, share_of(-1), share_of(-2)])
    downward = jnp.concatenate([root_inverse, share_of(1), share_of(1)])
    update, upward, downward = lax.optimization_barrier((update, upward, downward))
    update = exchange(update.reshape(layer, part, near * border_rows), ("front", "col"))
    upward = shift(upward, -1, False)
    downward = shift(downward, 1, False)

    low = lax.div(jnp.maximum(index, 0), high_count)
    owner = lax.rem(lax.div(low, halves) - lax.rem(row_id, near) + 1 + rows, rows)
    place = jnp.where(index < 0, -1, owner * halves + lax.rem(low, halves))
    high = lax.rem(index, high_count)
    landed = land(update, place, high, fronts, cols, low_count, high_count)
    landed = landed.reshape(far, near * halves * part, high_count)
    landed = lax.all_to_all(landed, "row", 0, 0, axis_index_groups=apart, tiled=True).sum(0)
    landed = landed.reshape(near, halves, part, high_count)

    twice = shift(upward, -1, False)
    shares = jnp.stack(
        [
            downward[share_rows : share_rows + part],
            share_of(0),
            upward[share_rows : share_rows + part],
            twice[share_rows + part :],
        ]
    )
    residual = shares.reshape(near, part, halves, high_count).transpose(0, 2, 1, 3) - landed
    residual = exchange(
        jnp.broadcast_to(residual[None], (layer, near, halves, part, high_count)), ("front", "col")
    )
    residual = residual.transpose(1, 0, 3, 2, 4).reshape(near, far * block, root_rows)

    window = (downward[:share_rows], root_inverse, upward[:share_rows], twice[:share_rows])
    root = sum(contract(residual[i], value, (1,), (1,)) for i, value in enumerate(window))
    root = root.reshape(far, block, share_rows)
    parts = []
    for offset in order:
        value = lax.dynamic_index_in_dim(root, lax.rem(far_id + offset, far), 0, keepdims=False)
        parts.append(shift(value, near * offset, False))
    root = lax.dynamic_index_in_dim(root, far_id, 0, keepdims=False)
    for value in parts:
        root = root + value
    return own.T[None], root.T


def solution(mesh):
    in_specs = (
        P("front", ("row", "col"), None),
        P("front", "col", "row"),
        P("front", "row", "col"),
        P("front", None),
        P("front", None),
        P("row", None),
        P(("front", "col"), "row"),
    )
    out_specs = (P("front", "col", "row"), P(("front", "col"), "row"))
    return jax.shard_map(local, mesh=mesh, in_specs=in_specs, out_specs=out_specs, check_vma=False)
```

```python
import functools

import jax
import jax.numpy as jnp
from jax import lax
from jax.experimental import pallas as pl
from jax.experimental.pallas import tpu as pltpu
from jax.sharding import PartitionSpec as P

HIGH = lax.Precision.HIGH


def contract(left, right, left_dims, right_dims):
    return lax.dot_general(
        left,
        right,
        ((left_dims, right_dims), ((), ())),
        precision=HIGH,
        preferred_element_type=jnp.float32,
    )


def exchange(blocks, axes):
    return lax.all_to_all(blocks, axes, split_axis=0, concat_axis=0, tiled=True)


def land_kernel(fronts, cols, border_rows, update_ref, out_ref):
    part = update_ref.shape[1]
    out_rows, high_count = out_ref.shape
    places = out_rows // part
    repeats = max(1, 8 // part)
    shape = (places // repeats, repeats * part, border_rows)
    place_iota = lax.broadcasted_iota(jnp.int32, shape, 0) * repeats
    place_iota = place_iota + lax.broadcasted_iota(jnp.int32, shape, 1) // part
    high_iota = lax.broadcasted_iota(jnp.int32, (high_count, border_rows), 0)
    total = None
    for front in range(fronts):
        value = update_ref[front * cols][:, :border_rows]
        for col in range(1, cols):
            value = value + update_ref[front * cols + col][:, :border_rows]
        codes = update_ref[front * cols][:, border_rows:]
        codes = jnp.concatenate([codes[row : row + 1] for row in range(part)], 1).astype(jnp.int32)
        place = jnp.where(codes < 0, -1, codes // high_count)
        high = codes % high_count
        value = jnp.concatenate([value] * repeats, 0)
        coarse = value.astype(jnp.bfloat16).astype(jnp.float32)
        at_high = jnp.where(high_iota == high, 1.0, 0.0).astype(jnp.bfloat16)
        at_place = place_iota == place[None]
        pieces = []
        for piece in (coarse, value - coarse):
            spread = jnp.where(at_place, piece[None], 0.0)
            pieces.append(spread.reshape(out_rows, border_rows).astype(jnp.bfloat16))
        landed = lax.dot_general(
            jnp.concatenate(pieces, 0),
            at_high,
            (((1,), (1,)), ((), ())),
            preferred_element_type=jnp.float32,
        )
        landed = landed[:out_rows] + landed[out_rows:]
        total = landed if total is None else total + landed
    out_ref[...] = total


def land(update, border_rows, fronts, cols, places, high_count):
    part = update.shape[1]
    return pl.pallas_call(
        functools.partial(land_kernel, fronts, cols, border_rows),
        out_shape=jax.ShapeDtypeStruct((places * part, high_count), jnp.float32),
        in_specs=[pl.BlockSpec(memory_space=pltpu.VMEM)],
        out_specs=pl.BlockSpec(memory_space=pltpu.VMEM),
        compiler_params=pltpu.CompilerParams(vmem_limit_bytes=32 * 1024 * 1024),
        cost_estimate=pl.CostEstimate(
            flops=4 * places * part * high_count * fronts * border_rows,
            bytes_accessed=4 * (update.size + places * part * high_count),
            transcendentals=0,
        ),
    )(update)


def local(
    child_rhs, pivot_inverse, border_factor, front_sizes, border_index, root_rhs, root_inverse
):
    rows = lax.axis_size("row")
    cols = lax.axis_size("col")
    fronts = lax.axis_size("front")
    layer = fronts * cols
    col_id = lax.axis_index("col")
    row_id = lax.axis_index("row")
    front_id = lax.axis_index("front")
    inverse = pivot_inverse[0]
    border = border_factor[0]
    pivot_rows = inverse.shape[0]
    border_rows = border.shape[0]
    root_rows, sources = root_rhs.shape
    near = 4
    part = sources // near // layer
    halves = 2
    low_count = rows * halves
    high_count = root_rows // halves

    far = rows // near
    block = sources // rows
    step = 1 - 2 * lax.rem(front_id, 2)

    def shift(value, distance, mirrored=True):
        pairs = []
        for front in range(fronts):
            by = -distance if mirrored and front % 2 else distance
            pairs += [(front * rows + z, front * rows + (z + by) % rows) for z in range(rows)]
        return lax.ppermute(value, ("front", "row"), pairs)

    def group_at(offset):
        return lax.rem(row_id + offset + near, near)

    index = []
    for offset in (0, step, -step, 2 * step):
        start = lax.rem(row_id + offset + rows, rows) * border_rows
        live = start + jnp.arange(border_rows, dtype=jnp.int32) < front_sizes[0, 1]
        piece = lax.dynamic_slice_in_dim(border_index[0], start, border_rows)
        index.append(jnp.where(live, piece, -1))
    index = jnp.concatenate(index)
    low = lax.div(jnp.maximum(index, 0), high_count)
    owner = lax.rem(lax.div(low, halves) - lax.rem(row_id, near) + 1 + rows, rows)
    code = (owner * halves + lax.rem(low, halves)) * high_count + lax.rem(index, high_count)
    code = jnp.where(index < 0, -1, code).astype(jnp.float32)
    code = jnp.tile(code.reshape(part, -1), (layer, 1))

    rhs = child_rhs[0].reshape(-1, far, near, block).transpose(2, 0, 1, 3)
    rhs = rhs.reshape(near, -1, far * block)
    rhs = jnp.stack(
        [
            lax.dynamic_index_in_dim(rhs, group_at(offset), 0, keepdims=False)
            for offset in (2, step, -step, 0)
        ]
    )
    border_above = shift(border, -1)
    border_below = shift(border, 1)
    rhs = lax.all_gather(rhs, "col", axis=1, tiled=True)

    def pivot_product(which):
        return contract(rhs[which], inverse, (0,), (1,))

    from_two = shift(pivot_product(0), -1)
    from_below = shift(pivot_product(1), 1)
    from_two, border_above, border_below = lax.optimization_barrier(
        (from_two, border_above, border_below)
    )
    above, border_sent = lax.optimization_barrier((pivot_product(2) + from_two, border_above))
    from_above = shift(above, -1)
    border_two = shift(border_sent, -1)
    near_sum = pivot_product(3) + from_below + from_above
    near_sum = near_sum.reshape(far, block, pivot_rows)
    far_id = lax.div(row_id, near)

    def far_block(offset):
        return lax.dynamic_index_in_dim(near_sum, lax.rem(far_id + offset, far), 0, keepdims=False)

    own = far_block(0)
    sent = []
    for offset in sorted(range(1, far), key=lambda offset: -min(offset, far - offset)):
        sent.append(shift(far_block(offset), near * offset, False))
    *sent, border_two = lax.optimization_barrier((*sent, border_two))
    for value in sent:
        own = own + value
    pivot_live = col_id * pivot_rows + jnp.arange(pivot_rows, dtype=jnp.int32) < front_sizes[0, 0]
    own = jnp.where(pivot_live[None, :], own, 0.0)

    apart = [[g + near * i for i in range(far)] for g in range(near)]
    solved = lax.all_gather(own, "row", axis_index_groups=apart, axis=0, tiled=True)
    window = (border, border_above, border_below, border_two)
    update = [contract(solved, value, (1,), (1,)) for value in window]
    update = jnp.concatenate([*update, code], 1)

    share = front_id * cols + col_id
    per_block = layer // far
    root_share = root_rhs.reshape(root_rows, far, near, per_block, part)
    root_share = lax.dynamic_index_in_dim(root_share, lax.div(share, per_block), 1, keepdims=False)
    root_share = lax.dynamic_index_in_dim(root_share, lax.rem(share, per_block), 2, keepdims=False)
    root_share = root_share.transpose(1, 2, 0)

    def share_of(offset):
        return lax.dynamic_index_in_dim(root_share, group_at(offset), 0, keepdims=False)

    share_rows = root_inverse.shape[0]
    upward = jnp.concatenate([root_inverse, share_of(-1), share_of(-2)])
    downward = jnp.concatenate([root_inverse, share_of(1), share_of(1)])
    update, upward, downward = lax.optimization_barrier(
        (update, shift(upward, -1, False), downward)
    )
    update = exchange(update.reshape(layer, part, -1), ("front", "col"))
    downward = shift(downward, 1, False)

    landed = land(update, near * border_rows, fronts, cols, low_count, high_count)
    landed = landed.reshape(far, near * halves * part, high_count)
    landed = lax.all_to_all(landed, "row", 0, 0, axis_index_groups=apart, tiled=True).sum(0)
    landed = landed.reshape(near, halves, part, high_count)

    twice = shift(upward, -1, False)
    shares = jnp.stack(
        [
            downward[share_rows : share_rows + part],
            share_of(0),
            upward[share_rows : share_rows + part],
            twice[share_rows + part :],
        ]
    )
    residual = shares.reshape(near, part, halves, high_count).transpose(0, 2, 1, 3) - landed
    residual = exchange(
        jnp.broadcast_to(residual[None], (layer, near, halves, part, high_count)), ("front", "col")
    )
    residual = residual.transpose(1, 0, 3, 2, 4).reshape(near, far * block, root_rows)

    window = (downward[:share_rows], root_inverse, upward[:share_rows], twice[:share_rows])
    root = sum(contract(residual[i], value, (1,), (1,)) for i, value in enumerate(window))
    root = root.reshape(far, block, share_rows)
    root = lax.all_to_all(root, "row", 0, 0, axis_index_groups=apart, tiled=True).sum(0)
    return own.T[None], root.T


def solution(mesh):
    in_specs = (
        P("front", ("row", "col"), None),
        P("front", "col", "row"),
        P("front", "row", "col"),
        P("front", None),
        P("front", None),
        P("row", None),
        P(("front", "col"), "row"),
    )
    out_specs = (P("front", "col", "row"), P(("front", "col"), "row"))
    return jax.shard_map(local, mesh=mesh, in_specs=in_specs, out_specs=out_specs, check_vma=False)
```
